32 devices in a mesh: group: 2 (over x), dp: 16 (over z, y, core).
Axes of the slice: x: 2, y: 2, z: 4, core: 2. Of those that a mesh axis runs over, the one named last changes fastest.
Arguments:
- features: bfloat16 [4096, 24576], P(('group', 'dp')), parts along dimension 0, may hold values from -120 to 120, as said below
- joining_gains: float32 [3, 8192], replicated, may hold values from 0.5 to 1.5
- destination: int32 [4096, 1], P(('group', 'dp')), parts along dimension 0, may hold values from 0 to 15; in each aligned block of 128 rows (0 to 127, 128 to 255, ...) at most 12 rows name the same one
- target_logits: bfloat16 [4096, 128], P(('group', 'dp')), parts along dimension 0, may hold values from -20 to 260, as said below
- joined_cotangent: bfloat16 [6144, 8192], P(('group', 'dp')), parts along dimension 0, may hold values from -0.4375 to 0.4375
Outputs:
- joined_input: bfloat16 [6144, 8192], P(('group', 'dp')), parts along dimension 0
- soft_labels: bfloat16 [6144, 128], P(('group', 'dp')), parts along dimension 0
- log_partition: float32 [6144], P(('group', 'dp')), parts along dimension 0
- gain_grad: float32 [6, 8192], P('group', 'dp'), parts along dimension 0
The draws below stay inside these ranges and needn't reach their ends.
There are 2 independent parts, one for each index of `group`. The reference program is written for one: setup_inputs(seed, part) draws one part's arguments, and reference() takes and returns one part's arrays. A program takes and returns all parts, laid end to end along the dimension named above; an argument that names none is the same for every part. Nothing has to cross between parts.
Inputs may be any that keep to these rules, and one draw needn't show every extreme that they name: `destination`: at most 12 tokens of one feature device name the same trainer; in every draw some feature device sends exactly 12 tokens to one trainer. `features`: Real-valued hidden states; rows and channels have unlike scales. `target_logits`: Real-valued logits.
All inputs are finite; a program needn't handle non-finite values.
Results may differ from the reference program's by a relative error of at most 0.001.
Values may be sent and summed in bfloat16 or wider, within the bound.
No kernel may reach another device: no remote copies, remote signals or barrier semaphores. Data moves between devices by JAX's collectives and lax.ppermute only.
A program may use at most 256 MiB of HBM per device.

```python
import math
import jax
import jax.numpy as jnp
import numpy as np
from jax import lax

D = 8192
LAYERS = 3
TOPK = 128
R_DEV = 128
CAP = 12
SLOTS = 192
TOKENS = 2048
N_DP = 16


def draw_features(key, part):
    key = jax.random.fold_in(key, 11)
    key_base, key_rows, key_cols = jax.random.split(key, 3)
    base_vals = jnp.clip(jax.random.normal(key_base, (TOKENS, LAYERS, D), jnp.float32), -4.0, 4.0)
    row_scale = jnp.exp(jax.random.uniform(key_rows, (TOKENS, LAYERS, 1), jnp.float32, 0.0, math.log(10.0)))
    col_scale = jnp.exp(jax.random.uniform(key_cols, (1, LAYERS, D), jnp.float32, 0.0, math.log(3.0)))
    return (base_vals * row_scale * col_scale).reshape(TOKENS, LAYERS * D).astype(jnp.bfloat16)


def draw_target_logits(key, part):
    key = jax.random.fold_in(key, 23)
    key_base = jax.random.fold_in(key, 0)
    logit_values = jnp.clip(3.0 * jax.random.normal(key_base, (TOKENS, TOPK), jnp.float32), -15.0, 15.0)
    return logit_values.astype(jnp.bfloat16)


def with_spikes(array, own_key, source, target, parts, factor):
    def block_of(dim):
        return (jnp.arange(array.shape[dim]) // (array.shape[dim] // parts)).reshape((-1,) + (1,) * (array.ndim - 1 - dim))

    near = jax.random.permutation(own_key, parts)[block_of(target)]
    other_side = (block_of(target) + parts // 2) % parts
    return jnp.where((block_of(source) == near) | (block_of(source) == other_side), factor * array, array)


def steps_of(rng, dims, cuts, low, high):
    level = 1.0
    for axis_at, shards_of in cuts:
        heights = jax.random.uniform(jax.random.fold_in(jax.random.fold_in(rng, 6), axis_at), (shards_of,), jnp.float32, low / len(cuts), high / len(cuts))
        level = level * jnp.repeat(jnp.exp(heights), dims[axis_at] // shards_of).reshape((-1,) + (1,) * (len(dims) - 1 - axis_at))
    return level


def assign_block(stream_key, own, number, rows, count, top, bound, lean):
    order = jax.random.permutation(stream_key, count)
    heavy_load, usual = load_shares(count, rows * top, bound, lean, True), load_shares(count, rows * top, bound, lean, False)
    places = jnp.arange(count)

    def named(sizes, offset_by):
        used = int((sizes > 0).sum())
        fixed = max(1, used // 4)
        shifted = fixed + (places - fixed + offset_by * (used - fixed)) % max(1, count - fixed)
        return jnp.zeros((count,), jnp.int32).at[order[jnp.where(places < fixed, places, shifted)]].set(jnp.asarray(sizes, jnp.int32))

    sizes = jnp.where(number % 4 == 0, named(heavy_load, number // 4), named(usual, number - number // 4 - 1))
    mixed = jax.random.permutation(jax.random.fold_in(own, 3), count)
    donor, receiver = mixed[0:count // 2 * 2:2], mixed[1:count // 2 * 2:2]
    room = jnp.minimum(sizes[donor] - 1, bound - sizes[receiver]) // 2
    room = jnp.where((donor == order[0]) | (receiver == order[0]) | (sizes[receiver] == 0), 0, jnp.maximum(room, 0))
    shifted = jax.random.randint(jax.random.fold_in(own, 4), (count // 2,), 0, 1 << 20) % (room + 1)
    sizes = sizes.at[donor].add(-shifted).at[receiver].add(shifted)
    labels = jnp.searchsorted(jnp.cumsum(sizes), jnp.arange(rows * top), side="right").astype(jnp.int32)
    grid = labels.reshape(top, rows).T
    grid = grid[jax.random.permutation(jax.random.fold_in(own, 1), rows)]
    offset_by = jax.random.randint(jax.random.fold_in(own, 2), (rows, 1), 0, top)
    return jnp.take_along_axis(grid, (jnp.arange(top)[None, :] + offset_by) % top, axis=1)


def load_shares(count, total, bound, slope, full):
    loads = [(1 << 20) // math.isqrt(standing ** slope) + 1 for standing in range(1, count + 1)]
    largest = bound if full else min(bound, max(-(-total // count), total * loads[0] // sum(loads)))
    least = 1 if total - largest >= count - 1 else 0
    holding, rest = [largest] + [least] * (count - 1), total - largest - least * (count - 1)
    while rest > 0:
        movable = [i for i in range(1, count) if holding[i] < largest] or [i for i in range(1, count) if holding[i] < bound]
        mass, budget = sum([loads[i] for i in movable]), rest
        for i in movable:
            more = min(bound - holding[i], max(1, budget * loads[i] // mass), rest)
            holding[i] = holding[i] + more
            rest = rest - more
    return np.array(holding)


def noise_with(own_key, extent, spread, bound, cuts, heavy, kind=jnp.bfloat16):
    array = spread * jax.random.normal(own_key, extent, jnp.float32)
    if cuts:
        array = array * steps_of(own_key, extent, cuts, -0.22, 0.18)
    return jnp.clip(with_spikes(array, jax.random.fold_in(own_key, 3), *heavy), -bound, bound).astype(kind)


def setup_inputs(seed: int = 0, part: int = 0) -> dict:
    splits = jax.random.split(jax.random.key(seed), 6)
    part_keys = jax.random.split(jax.random.fold_in(splits[5], part), 6)
    features = draw_features(jax.random.fold_in(jax.random.fold_in(splits[5], part), 71), part)
    joining_gains = jnp.clip(1.0 + 0.1 * jax.random.normal(splits[1], (LAYERS, D), jnp.float32), 0.5, 1.5)
    destination_keys = jax.random.split(jax.random.fold_in(part_keys[2], 1), TOKENS // R_DEV)
    destination_turns = jax.random.permutation(jax.random.fold_in(part_keys[2], 3), TOKENS // R_DEV)
    destination = jax.vmap(lambda own, number: assign_block(jax.random.fold_in(part_keys[2], 2), own, number, R_DEV, N_DP, 1, CAP, 2))(destination_keys, destination_turns).reshape((TOKENS, 1))
    target_logits = draw_target_logits(jax.random.fold_in(jax.random.fold_in(splits[5], part), 71), part)
    joined_cotangent = noise_with(part_keys[4], (N_DP * SLOTS, D), 0.02, 0.4375, ((0, 16),), (0, 1, 16, 2.0))
    return {"features": features, "joining_gains": joining_gains, "destination": destination, "target_logits": target_logits, "joined_cotangent": joined_cotangent}


eps = 1e-06

def normalize(row_block, joining_gains):
    widened = row_block.astype(jnp.float32).reshape(row_block.shape[0], LAYERS, D)
    scaled = widened * lax.rsqrt(lax.optimization_barrier(jnp.mean(widened * widened, axis=2, keepdims=True)) + eps)
    joined_vals = lax.optimization_barrier(jnp.sum(scaled * joining_gains.astype(jnp.float32)[None], axis=1))
    return (scaled, joined_vals)

def slot_of(destination):
    dest_grid = destination[:, 0].reshape(N_DP, R_DEV)
    onehot = (dest_grid[:, :, None] == jnp.arange(N_DP, dtype=jnp.int32)[None, None, :]).astype(jnp.int32)
    before = (jnp.cumsum(onehot, axis=1) - onehot).astype(jnp.int32)
    rank_in = lax.optimization_barrier(jnp.sum(before * onehot, axis=2)).astype(jnp.int32)
    source = jnp.arange(N_DP, dtype=jnp.int32)[:, None]
    return (dest_grid * SLOTS + source * CAP + rank_in).reshape(TOKENS).astype(jnp.int32)

def reference(features, joining_gains, destination, target_logits, joined_cotangent):
    slot_index = slot_of(destination)
    row_cot = joined_cotangent[slot_index]

    def per_block(block_pair):
        row_block, cot_block = block_pair
        scaled, joined_vals = normalize(row_block, joining_gains)
        partial_value = lax.optimization_barrier(jnp.sum(scaled * cot_block.astype(jnp.float32)[:, None, :], axis=0))
        return (joined_vals.astype(jnp.bfloat16), partial_value)
    joined_blocks, partials = lax.map(per_block, (features.reshape(N_DP, R_DEV, LAYERS * D), row_cot.reshape(N_DP, R_DEV, D)))
    gain_grad = lax.optimization_barrier(jnp.sum(partials, axis=0))
    joined_input = jnp.zeros((N_DP * SLOTS, D), jnp.bfloat16).at[slot_index].set(joined_blocks.reshape(TOKENS, D))
    slot_logits = jnp.zeros((N_DP * SLOTS, TOPK), jnp.bfloat16).at[slot_index].set(target_logits)
    logit_values = slot_logits.astype(jnp.float32)
    log_partition = jax.nn.logsumexp(logit_values, axis=1)
    soft_labels = jnp.exp(logit_values - log_partition[:, None]).astype(jnp.bfloat16)
    return (joined_input, soft_labels, log_partition, gain_grad)
```

```python
import functools

import jax
import jax.numpy as jnp
from jax import lax
from jax.experimental import pallas as pl
from jax.experimental.pallas import tpu as pltpu
from jax.sharding import PartitionSpec as P

eps = 1e-06
SUB = 8
GROUP = 1024
LANES = 128
VMEM_LIMIT = 40 * 1024 * 1024


def pieces_of(capacity):
    found, first = [], 0
    for size in (8, 4, 2, 1):
        while capacity - first >= size:
            found.append((first, size, SUB // size))
            first += size
    return found


def iota(shape, dim):
    return lax.broadcasted_iota(jnp.int32, shape, dim)


def ranks_of(dest_row):
    tokens = dest_row.shape[1]
    across = jnp.broadcast_to(dest_row.astype(jnp.float32), (tokens, tokens))
    down = across.T
    same = across == down
    row, col = iota((tokens, tokens), 0), iota((tokens, tokens), 1)
    rank_row = jnp.sum(jnp.where(same & (row < col), 1.0, 0.0), axis=0, keepdims=True).astype(jnp.int32)
    rank_col = jnp.sum(jnp.where(same & (col < row), 1.0, 0.0), axis=1, keepdims=True).astype(jnp.int32)
    return dest_row, rank_row, down[:, :1].astype(jnp.int32), rank_col


def spread(target, rank, first, size, h):
    inside = (rank >= first) & (rank < first + size)
    return jnp.where(inside, target * SUB + h * size + rank - first, -1)


def hot(cond):
    return jnp.where(cond, 1.0, 0.0).astype(jnp.bfloat16)


def select(matrix, values):
    return jnp.dot(matrix, values, preferred_element_type=jnp.float32).astype(jnp.bfloat16)


def pack_matrices(target, rank, groups, capacity):
    shape = (groups * SUB, target.shape[1])
    out = []
    for first, size, splits in pieces_of(capacity):
        parts = [hot(iota(shape, 0) == spread(target, rank, first, size, h)) for h in range(splits)]
        out.append(parts[0] if splits == 1 else jnp.concatenate(parts, axis=1))
    return out


def pack_group(values, matrices, capacity):
    out = []
    for (_, _, splits), matrix in zip(pieces_of(capacity), matrices):
        wide = values.shape[1] // splits
        stacked = values if splits == 1 else jnp.concatenate([values[:, h * wide : (h + 1) * wide] for h in range(splits)], axis=0)
        out.append(select(matrix, stacked))
    return out


def unpack_matrices(target, rank, groups, capacity):
    shape = (target.shape[0], groups * SUB)
    runs = pieces_of(capacity)
    finest = max(splits for _, _, splits in runs)
    out = []
    for b in range(finest):
        parts = [hot(iota(shape, 1) == spread(target, rank, first, size, b * splits // finest)) for first, size, splits in runs]
        out.append(jnp.concatenate(parts, axis=1))
    return out


def unpack_group(packed, matrices, capacity, group):
    runs = pieces_of(capacity)
    finest = max(splits for _, _, splits in runs)
    wide = group // finest
    out = []
    for b in range(finest):
        parts, base = [], 0
        for _, _, splits in runs:
            own = group // splits
            at = base + b * wide - (b * splits // finest) * own
            parts.append(packed[:, at : at + wide])
            base += own
        out.append(jnp.dot(matrices[b], jnp.concatenate(parts, axis=0), preferred_element_type=jnp.float32))
    return out


def cols(ref, g, wide):
    return ref.at[:, g * wide : (g + 1) * wide]


def cot_kernel(groups, capacity, dest_ref, logit_ref, cot_hbm, out_hbm, cot_v, out_v, log_v, in_sem, out_sem, log_sem):
    count, slots, group = cot_v.shape
    packed = out_v.shape[2]
    loads = [pltpu.make_async_copy(cols(cot_hbm, g, group), cot_v.at[g], in_sem.at[g]) for g in range(count)]
    stores = [pltpu.make_async_copy(out_v.at[g], cols(out_hbm, g, packed), out_sem.at[g]) for g in range(count)]
    for load in loads:
        load.start()
    target, rank, _, _ = ranks_of(dest_ref[...])
    shape = (groups * SUB, target.shape[1])
    for m in range(log_v.shape[1] // LANES):
        place = hot(iota(shape, 0) == spread(target, rank, m * SUB, SUB, 0))
        log_v[:, m * LANES : (m + 1) * LANES] = select(place, logit_ref[...])
    log_store = pltpu.make_async_copy(log_v, out_hbm.at[:, count * packed : count * packed + log_v.shape[1]], log_sem)
    log_store.start()
    slot = iota((1, slots), 1)
    matrices = pack_matrices(slot // capacity, slot % capacity, groups, capacity)
    for g in range(count):
        loads[g].wait()
        base = 0
        for block in pack_group(cot_v[g], matrices, capacity):
            out_v[g, :, base : base + block.shape[1]] = block
            base += block.shape[1]
        stores[g].start()
    for store in stores:
        store.wait()
    log_store.wait()


def join_kernel(groups, capacity, dest_ref, gain_ref, feat_hbm, out_hbm, inv_ref, feat_v, out_v, in_sem, out_sem):
    layers, count, tokens, group = feat_v.shape
    width = count * group
    packed = out_v.shape[2]
    loads = [
        [pltpu.make_async_copy(cols(feat_hbm, l * count + g, group), feat_v.at[l, g], in_sem.at[l, g]) for g in range(count)]
        for l in range(layers)
    ]
    stores = [pltpu.make_async_copy(out_v.at[g], cols(out_hbm, g, packed), out_sem.at[g]) for g in range(count)]
    for row in loads:
        for load in row:
            load.start()
    target, rank, _, _ = ranks_of(dest_ref[...])
    matrices = pack_matrices(target, rank, groups, capacity)
    lane = iota((tokens, LANES), 1)
    inv_all = jnp.zeros((tokens, LANES), jnp.float32)
    inverse = []
    for l in range(layers):
        total = jnp.zeros((tokens, LANES), jnp.float32)
        for g in range(count):
            loads[l][g].wait()
            for k in range(group // LANES):
                x = feat_v[l, g, :, k * LANES : (k + 1) * LANES].astype(jnp.float32)
                total = total + x * x
        mean = jnp.sum(total, axis=1, keepdims=True) / width
        inv = lax.rsqrt(mean + eps)
        inverse.append(inv)
        inv_all = jnp.where(lane == l, inv, inv_all)
    inv_ref[...] = inv_all
    for g in range(count):
        joined = None
        for l in range(layers):
            term = feat_v[l, g].astype(jnp.float32) * inverse[l] * gain_ref[l : l + 1, g * group : (g + 1) * group]
            joined = term if joined is None else joined + term
        base = 0
        for block in pack_group(joined.astype(jnp.bfloat16), matrices, capacity):
            out_v[g, :, base : base + block.shape[1]] = block
            base += block.shape[1]
        stores[g].start()
    for store in stores:
        store.wait()


def grad_kernel(
    groups, capacity, dest_ref, inv_ref, feat_hbm, got_hbm, grad_ref, soft_ref, part_ref, feat_v, got_v, log_v, in_sem, got_sem, log_sem
):
    layers, count, tokens, group = feat_v.shape
    packed = got_v.shape[2]
    own = grad_ref.shape[1] // layers
    log_load = pltpu.make_async_copy(got_hbm.at[:, count * packed : count * packed + log_v.shape[1]], log_v, log_sem)
    log_load.start()
    gots = [pltpu.make_async_copy(cols(got_hbm, g, packed), got_v.at[g], got_sem.at[g]) for g in range(count)]
    loads = [
        [pltpu.make_async_copy(cols(feat_hbm, l * count + g, group), feat_v.at[l, g], in_sem.at[l, g]) for g in range(count)]
        for l in range(layers)
    ]
    for g in range(count):
        gots[g].start()
        for l in range(layers):
            loads[l][g].start()
    _, _, target, rank = ranks_of(dest_ref[...])
    matrices = unpack_matrices(target, rank, groups, capacity)
    for g in range(count):
        gots[g].wait()
        for l in range(layers):
            loads[l][g].wait()
        blocks = unpack_group(got_v[g], matrices, capacity, group)
        wide = group // len(blocks)
        for b, cot in enumerate(blocks):
            step = min(own, wide)
            for l in range(layers):
                x = feat_v[l, g, :, b * wide : (b + 1) * wide].astype(jnp.float32)
                part = jnp.sum(x * inv_ref[:, l : l + 1] * cot, axis=0, keepdims=True)
                for u in range(wide // step):
                    at = g * group + b * wide + u * step
                    lo = l * own + at % own
                    grad_ref[at // own : at // own + 1, lo : lo + step] = part[:, u * step : (u + 1) * step]
    log_load.wait()
    slots = soft_ref.shape[0]
    slot = iota((slots, 1), 0)
    target, rank = slot // capacity, slot % capacity
    shape = (slots, groups * SUB)
    logits = jnp.zeros((slots, LANES), jnp.float32)
    for m in range(log_v.shape[1] // LANES):
        place = hot(iota(shape, 1) == spread(target, rank, m * SUB, SUB, 0))
        logits = logits + jnp.dot(place, log_v[:, m * LANES : (m + 1) * LANES], preferred_element_type=jnp.float32)
    top = jnp.max(logits, axis=1, keepdims=True)
    partition = top + jnp.log(jnp.sum(jnp.exp(logits - top), axis=1, keepdims=True))
    part_ref[...] = partition
    soft_ref[...] = jnp.exp(logits - partition).astype(jnp.bfloat16)


def place_kernel(groups, capacity, got_hbm, out_hbm, got_v, out_v, in_sem, out_sem):
    count, slots, group = out_v.shape
    packed = got_v.shape[2]
    loads = [pltpu.make_async_copy(cols(got_hbm, g, packed), got_v.at[g], in_sem.at[g]) for g in range(count)]
    stores = [pltpu.make_async_copy(out_v.at[g], cols(out_hbm, g, group), out_sem.at[g]) for g in range(count)]
    for load in loads:
        load.start()
    slot = iota((slots, 1), 0)
    matrices = unpack_matrices(slot // capacity, slot % capacity, groups, capacity)
    for g in range(count):
        loads[g].wait()
        blocks = unpack_group(got_v[g], matrices, capacity, group)
        wide = group // len(blocks)
        for b, block in enumerate(blocks):
            out_v[g, :, b * wide : (b + 1) * wide] = block.astype(jnp.bfloat16)
        stores[g].start()
    for store in stores:
        store.wait()


vmem = pl.BlockSpec(memory_space=pltpu.VMEM)
hbm = pl.BlockSpec(memory_space=pl.ANY)


def call(kernel, name, ins, out_shape, outs, scratch, moved, flops):
    return pl.pallas_call(
        kernel,
        out_shape=out_shape,
        in_specs=ins,
        out_specs=outs,
        scratch_shapes=scratch,
        compiler_params=pltpu.CompilerParams(vmem_limit_bytes=VMEM_LIMIT),
        cost_estimate=pl.CostEstimate(flops=flops, bytes_accessed=moved, transcendentals=0),
        name=name,
    )


def reduce_rows(rows, axis):
    size = lax.axis_size(axis)
    me = lax.axis_index(axis)
    half = size // 2
    while half >= 1:
        upper = (me // half) % 2 == 1
        low, high = rows[:half], rows[half:]
        sent = jnp.where(upper, low, high)
        kept = jnp.where(upper, high, low)
        rows = kept + lax.ppermute(sent, axis, [(i, i ^ half) for i in range(size)])
        half //= 2
    return rows


def per_device(features, joining_gains, destination, target_logits, joined_cotangent):
    groups = lax.axis_size("dp")
    slots, width = joined_cotangent.shape
    capacity = slots // groups
    layers = joining_gains.shape[0]
    tokens, kept = target_logits.shape
    count = width // GROUP
    packed = GROUP * capacity // SUB
    rows = groups * SUB
    log_wide = -(-capacity // SUB) * kept
    bf16, f32, dma = jnp.bfloat16, jnp.float32, pltpu.SemaphoreType.DMA
    shape = jax.ShapeDtypeStruct
    dest_row = destination.reshape(1, tokens)

    cot_send = call(
        functools.partial(cot_kernel, groups, capacity),
        "pack_cotangent",
        [vmem, vmem, hbm],
        shape((rows, count * packed + log_wide), bf16),
        hbm,
        [
            pltpu.VMEM((count, slots, GROUP), bf16),
            pltpu.VMEM((count, rows, packed), bf16),
            pltpu.VMEM((rows, log_wide), bf16),
            dma((count,)),
            dma((count,)),
            dma,
        ],
        4 * slots * width,
        2 * rows * slots * width * 2,
    )(dest_row, target_logits, joined_cotangent)
    cot_got = lax.all_to_all(cot_send, "dp", split_axis=0, concat_axis=0, tiled=True)

    join_send, inverse = call(
        functools.partial(join_kernel, groups, capacity),
        "join_layers",
        [vmem, vmem, hbm],
        (shape((rows, count * packed), bf16), shape((tokens, LANES), f32)),
        (hbm, vmem),
        [
            pltpu.VMEM((layers, count, tokens, GROUP), bf16),
            pltpu.VMEM((count, rows, packed), bf16),
            dma((layers, count)),
            dma((count,)),
        ],
        2 * layers * tokens * width + 2 * slots * width,
        2 * rows * tokens * width * 2,
    )(dest_row, joining_gains, features)
    join_got = lax.all_to_all(join_send, "dp", split_axis=0, concat_axis=0, tiled=True)

    partial_rows, soft_labels, log_partition = call(
        functools.partial(grad_kernel, groups, capacity),
        "gain_partials",
        [vmem, vmem, hbm, hbm],
        (shape((groups, layers * width // groups), f32), shape((slots, kept), bf16), shape((slots, 1), f32)),
        (vmem, vmem, vmem),
        [
            pltpu.VMEM((layers, count, tokens, GROUP), bf16),
            pltpu.VMEM((count, rows, packed), bf16),
            pltpu.VMEM((rows, log_wide), bf16),
            dma((layers, count)),
            dma((count,)),
            dma,
        ],
        2 * layers * tokens * width + 2 * slots * width,
        2 * rows * tokens * width * 2,
    )(dest_row, inverse, features, cot_got)
    gain_grad = reduce_rows(partial_rows, "dp").reshape(layers, width // groups)

    joined_input = call(
        functools.partial(place_kernel, groups, capacity),
        "place_joined",
        [hbm],
        shape((slots, width), bf16),
        hbm,
        [pltpu.VMEM((count, rows, packed), bf16), pltpu.VMEM((count, slots, GROUP), bf16), dma((count,)), dma((count,))],
        4 * slots * width,
        2 * rows * slots * width * 2,
    )(join_got)
    return (joined_input, soft_labels, log_partition[:, 0], gain_grad)


def solution(mesh):
    placed = (
        P(("group", "dp"), None),
        P(),
        P(("group", "dp"), None),
        P(("group", "dp"), None),
        P(("group", "dp"), None),
    )
    return jax.shard_map(
        per_device,
        mesh=mesh,
        in_specs=placed,
        out_specs=(
            P(("group", "dp"), None),
            P(("group", "dp"), None),
            P(("group", "dp")),
            P("group", "dp"),
        ),
        check_vma=False,
    )
```

```python
import functools

import jax
import jax.numpy as jnp
from jax import lax
from jax.experimental import pallas as pl
from jax.experimental.pallas import tpu as pltpu
from jax.sharding import PartitionSpec as P

eps = 1e-06
SUB = 8
GROUP = 2048
LANES = 128
VMEM_LIMIT = 20 * 1024 * 1024
VMEM_WHOLE = 56 * 1024 * 1024


def pieces_of(capacity):
    found, first = [], 0
    for size in (8, 4, 2, 1):
        while capacity - first >= size:
            found.append((first, size, SUB // size))
            first += size
    return found


def radices(size):
    found = []
    while size > 1:
        found.append(4 if size % 4 == 0 else 2)
        size //= found[-1]
    return found


def exchange_order(size):
    order = []
    for device in range(size):
        row, rest = 0, device
        for radix in radices(size):
            row, rest = row * radix + rest % radix, rest // radix
        order.append(row)
    return order


def iota(shape, dim):
    return lax.broadcasted_iota(jnp.int32, shape, dim)


def ranks_of(dest_row):
    tokens = dest_row.shape[1]
    across = jnp.broadcast_to(dest_row.astype(jnp.float32), (tokens, tokens))
    down = across.T
    same = across == down
    row, col = iota((tokens, tokens), 0), iota((tokens, tokens), 1)
    rank_row = jnp.sum(jnp.where(same & (row < col), 1.0, 0.0), axis=0, keepdims=True).astype(jnp.int32)
    rank_col = jnp.sum(jnp.where(same & (col < row), 1.0, 0.0), axis=1, keepdims=True).astype(jnp.int32)
    return dest_row, rank_row, down[:, :1].astype(jnp.int32), rank_col


def spread(target, rank, first, size, h):
    inside = (rank >= first) & (rank < first + size)
    return jnp.where(inside, target * SUB + h * size + rank - first, -1)


def hot(cond):
    return jnp.where(cond, 1.0, 0.0).astype(jnp.bfloat16)


def select(matrix, values):
    return jnp.dot(matrix, values, preferred_element_type=jnp.float32).astype(jnp.bfloat16)


def pack_matrices(target, rank, groups, capacity):
    shape = (groups * SUB, target.shape[1])
    out = []
    for first, size, splits in pieces_of(capacity):
        parts = [hot(iota(shape, 0) == spread(target, rank, first, size, h)) for h in range(splits)]
        out.append(parts[0] if splits == 1 else jnp.concatenate(parts, axis=1))
    return out


def pack_group(values, matrices, capacity):
    out = []
    for (_, _, splits), matrix in zip(pieces_of(capacity), matrices):
        wide = values.shape[1] // splits
        stacked = values if splits == 1 else jnp.concatenate([values[:, h * wide : (h + 1) * wide] for h in range(splits)], axis=0)
        out.append(select(matrix, stacked))
    return out


def unpack_matrices(target, rank, groups, capacity):
    shape = (target.shape[0], groups * SUB)
    runs = pieces_of(capacity)
    finest = max(splits for _, _, splits in runs)
    out = []
    for b in range(finest):
        parts = [hot(iota(shape, 1) == spread(target, rank, first, size, b * splits // finest)) for first, size, splits in runs]
        out.append(jnp.concatenate(parts, axis=1))
    return out


def unpack_group(packed, matrices, capacity, group):
    runs = pieces_of(capacity)
    finest = max(splits for _, _, splits in runs)
    wide = group // finest
    out = []
    for b in range(finest):
        parts, base = [], 0
        for _, _, splits in runs:
            own = group // splits
            at = base + b * wide - (b * splits // finest) * own
            parts.append(packed[:, at : at + wide])
            base += own
        out.append(jnp.dot(matrices[b], jnp.concatenate(parts, axis=0), preferred_element_type=jnp.float32))
    return out


def cols(ref, g, wide):
    return ref.at[:, g * wide : (g + 1) * wide]


def cot_kernel(
    groups, capacity, dest_hbm, logit_hbm, cot_hbm, out_hbm, dest_v, logit_v, cot_v, out_v, log_v, dest_sem, logit_sem, in_sem, out_sem, log_sem
):
    count, slots, group = cot_v.shape
    packed = out_v.shape[2]
    loads = [pltpu.make_async_copy(cols(cot_hbm, g, group), cot_v.at[g], in_sem.at[g]) for g in range(count)]
    stores = [pltpu.make_async_copy(out_v.at[g], cols(out_hbm, g, packed), out_sem.at[g]) for g in range(count)]
    dest_load = pltpu.make_async_copy(dest_hbm, dest_v, dest_sem)
    logit_load = pltpu.make_async_copy(logit_hbm, logit_v, logit_sem)
    dest_load.start()
    logit_load.start()
    for load in loads:
        load.start()
    dest_load.wait()
    target, rank, _, _ = ranks_of(dest_v[...])
    shape = (groups * SUB, target.shape[1])
    logit_load.wait()
    for m in range(log_v.shape[1] // LANES):
        place = hot(iota(shape, 0) == spread(target, rank, m * SUB, SUB, 0))
        log_v[:, m * LANES : (m + 1) * LANES] = select(place, logit_v[...])
    log_store = pltpu.make_async_copy(log_v, out_hbm.at[:, count * packed : count * packed + log_v.shape[1]], log_sem)
    log_store.start()
    slot = iota((1, slots), 1)
    matrices = pack_matrices(slot // capacity, slot % capacity, groups, capacity)
    for g in range(count):
        loads[g].wait()
        base = 0
        for block in pack_group(cot_v[g], matrices, capacity):
            out_v[g, :, base : base + block.shape[1]] = block
            base += block.shape[1]
        stores[g].start()
    for store in stores:
        store.wait()
    log_store.wait()


def join_kernel(groups, capacity, dest_ref, gain_ref, feat_hbm, out_hbm, inv_ref, feat_v, out_v, in_sem, out_sem):
    layers, count, tokens, group = feat_v.shape
    width = count * group
    packed = out_v.shape[2]
    loads = [
        [pltpu.make_async_copy(cols(feat_hbm, l * count + g, group), feat_v.at[l, g], in_sem.at[l, g]) for g in range(count)]
        for l in range(layers)
    ]
    stores = [pltpu.make_async_copy(out_v.at[g], cols(out_hbm, g, packed), out_sem.at[g]) for g in range(count)]
    for row in loads:
        for load in row:
            load.start()
    target, rank, _, _ = ranks_of(dest_ref[...])
    matrices = pack_matrices(target, rank, groups, capacity)
    lane = iota((tokens, LANES), 1)
    inv_all = jnp.zeros((tokens, LANES), jnp.float32)
    inverse = []
    for l in range(layers):
        total = jnp.zeros((tokens, LANES), jnp.float32)
        for g in range(count):
            loads[l][g].wait()
            for k in range(group // LANES):
                x = feat_v[l, g, :, k * LANES : (k + 1) * LANES].astype(jnp.float32)
                total = total + x * x
        mean = jnp.sum(total, axis=1, keepdims=True) / width
        inv = lax.rsqrt(mean + eps)
        inverse.append(inv)
        inv_all = jnp.where(lane == l, inv, inv_all)
    inv_ref[...] = inv_all
    for g in range(count):
        joined = None
        for l in range(layers):
            term = feat_v[l, g].astype(jnp.float32) * inverse[l] * gain_ref[l : l + 1, g * group : (g + 1) * group]
            joined = term if joined is None else joined + term
        base = 0
        for block in pack_group(joined.astype(jnp.bfloat16), matrices, capacity):
            out_v[g, :, base : base + block.shape[1]] = block
            base += block.shape[1]
        stores[g].start()
    for store in stores:
        store.wait()


def grad_kernel(
    groups, capacity, dest_ref, inv_ref, feat_hbm, got_hbm, grad_ref, soft_ref, part_ref, feat_v, got_v, log_v, in_sem, got_sem, log_sem
):
    layers, count, tokens, group = feat_v.shape
    packed = got_v.shape[2]
    own = grad_ref.shape[1] // layers
    order = exchange_order(groups)
    log_load = pltpu.make_async_copy(got_hbm.at[:, count * packed : count * packed + log_v.shape[1]], log_v, log_sem)
    log_load.start()
    gots = [pltpu.make_async_copy(cols(got_hbm, g, packed), got_v.at[g], got_sem.at[g]) for g in range(count)]
    loads = [
        [pltpu.make_async_copy(cols(feat_hbm, l * count + g, group), feat_v.at[l, g], in_sem.at[l, g]) for g in range(count)]
        for l in range(layers)
    ]
    for g in range(count):
        gots[g].start()
        for l in range(layers):
            loads[l][g].start()
    _, _, target, rank = ranks_of(dest_ref[...])
    matrices = unpack_matrices(target, rank, groups, capacity)
    for g in range(count):
        gots[g].wait()
        for l in range(layers):
            loads[l][g].wait()
        blocks = unpack_group(got_v[g], matrices, capacity, group)
        wide = group // len(blocks)
        for b, cot in enumerate(blocks):
            step = min(own, wide)
            for l in range(layers):
                x = feat_v[l, g, :, b * wide : (b + 1) * wide].astype(jnp.float32)
                part = jnp.sum(x * inv_ref[:, l : l + 1] * cot, axis=0, keepdims=True)
                for u in range(wide // step):
                    at = g * group + b * wide + u * step
                    lo = l * own + at % own
                    row = order[at // own]
                    grad_ref[row : row + 1, lo : lo + step] = part[:, u * step : (u + 1) * step]
    log_load.wait()
    slots = soft_ref.shape[0]
    slot = iota((slots, 1), 0)
    target, rank = slot // capacity, slot % capacity
    shape = (slots, groups * SUB)
    logits = jnp.zeros((slots, LANES), jnp.float32)
    for m in range(log_v.shape[1] // LANES):
        place = hot(iota(shape, 1) == spread(target, rank, m * SUB, SUB, 0))
        logits = logits + jnp.dot(place, log_v[:, m * LANES : (m + 1) * LANES], preferred_element_type=jnp.float32)
    top = jnp.max(logits, axis=1, keepdims=True)
    partition = top + jnp.log(jnp.sum(jnp.exp(logits - top), axis=1, keepdims=True))
    part_ref[...] = partition
    soft_ref[...] = jnp.exp(logits - partition).astype(jnp.bfloat16)


def place_kernel(groups, capacity, got_hbm, out_hbm, got_v, out_v, in_sem, out_sem):
    count, slots, group = out_v.shape
    packed = got_v.shape[2]
    loads = [pltpu.make_async_copy(cols(got_hbm, g, packed), got_v.at[g], in_sem.at[g]) for g in range(count)]
    stores = [pltpu.make_async_copy(out_v.at[g], cols(out_hbm, g, group), out_sem.at[g]) for g in range(count)]
    for load in loads:
        load.start()
    slot = iota((slots, 1), 0)
    matrices = unpack_matrices(slot // capacity, slot % capacity, groups, capacity)
    for g in range(count):
        loads[g].wait()
        blocks = unpack_group(got_v[g], matrices, capacity, group)
        wide = group // len(blocks)
        for b, block in enumerate(blocks):
            out_v[g, :, b * wide : (b + 1) * wide] = block.astype(jnp.bfloat16)
        stores[g].start()
    for store in stores:
        store.wait()


vmem = pl.BlockSpec(memory_space=pltpu.VMEM)
hbm = pl.BlockSpec(memory_space=pltpu.HBM)
anywhere = pl.BlockSpec(memory_space=pl.ANY)


def call(kernel, name, ins, out_shape, outs, scratch, moved, flops, limit=VMEM_LIMIT):
    return pl.pallas_call(
        kernel,
        out_shape=out_shape,
        in_specs=ins,
        out_specs=outs,
        scratch_shapes=scratch,
        compiler_params=pltpu.CompilerParams(vmem_limit_bytes=limit),
        cost_estimate=pl.CostEstimate(flops=flops, bytes_accessed=moved, transcendentals=0),
        name=name,
    )


def reduce_rows(rows, axis):
    size = lax.axis_size(axis)
    me = lax.axis_index(axis)
    stride = 1
    for radix in radices(size):
        part = rows.shape[0] // radix
        digit = lax.rem(lax.div(me, stride), radix)
        total = lax.dynamic_slice_in_dim(rows, digit * part, part, 0)
        got = []
        for m in range(1, radix):
            sent = lax.dynamic_slice_in_dim(rows, (digit ^ m) * part, part, 0)
            got.append(lax.ppermute(sent, axis, [(i, i ^ (m * stride)) for i in range(size)]))
        for value in got:
            total = total + value
        rows = total
        stride *= radix
    return rows


def per_device(features, joining_gains, destination, target_logits, joined_cotangent):
    groups = lax.axis_size("dp")
    slots, width = joined_cotangent.shape
    capacity = slots // groups
    layers = joining_gains.shape[0]
    tokens, kept = target_logits.shape
    count = width // GROUP
    packed = GROUP * capacity // SUB
    rows = groups * SUB
    log_wide = -(-capacity // SUB) * kept
    bf16, f32, dma = jnp.bfloat16, jnp.float32, pltpu.SemaphoreType.DMA
    shape = jax.ShapeDtypeStruct
    dest_row = destination.reshape(1, tokens)

    cot_send = call(
        functools.partial(cot_kernel, groups, capacity),
        "pack_cotangent",
        [hbm, hbm, hbm],
        shape((rows, count * packed + log_wide), bf16),
        hbm,
        [
            pltpu.VMEM((1, tokens), jnp.int32),
            pltpu.VMEM((tokens, kept), bf16),
            pltpu.VMEM((count, slots, GROUP), bf16),
            pltpu.VMEM((count, rows, packed), bf16),
            pltpu.VMEM((rows, log_wide), bf16),
            dma,
            dma,
            dma((count,)),
            dma((count,)),
            dma,
        ],
        4 * slots * width,
        2 * rows * slots * width * 2,
        VMEM_WHOLE,
    )(dest_row, target_logits, joined_cotangent)
    cot_got = lax.all_to_all(cot_send, "dp", split_axis=0, concat_axis=0, tiled=True)

    join_send, inverse = call(
        functools.partial(join_kernel, groups, capacity),
        "join_layers",
        [vmem, vmem, hbm],
        (shape((rows, count * packed), bf16), shape((tokens, LANES), f32)),
        (hbm, vmem),
        [
            pltpu.VMEM((layers, count, tokens, GROUP), bf16),
            pltpu.VMEM((count, rows, packed), bf16),
            dma((layers, count)),
            dma((count,)),
        ],
        2 * layers * tokens * width + 2 * slots * width,
        2 * rows * tokens * width * 2,
    )(dest_row, joining_gains, features)
    join_got = lax.all_to_all(join_send, "dp", split_axis=0, concat_axis=0, tiled=True)

    partial_rows, soft_labels, log_partition = call(
        functools.partial(grad_kernel, groups, capacity),
        "gain_partials",
        [vmem, vmem, hbm, anywhere],
        (shape((groups, layers * width // groups), f32), shape((slots, kept), bf16), shape((slots, 1), f32)),
        (vmem, vmem, vmem),
        [
            pltpu.VMEM((layers, count, tokens, GROUP), bf16),
            pltpu.VMEM((count, rows, packed), bf16),
            pltpu.VMEM((rows, log_wide), bf16),
            dma((layers, count)),
            dma((count,)),
            dma,
        ],
        2 * layers * tokens * width + 2 * slots * width,
        2 * rows * tokens * width * 2,
    )(dest_row, inverse, features, cot_got)
    gain_grad = reduce_rows(partial_rows, "dp").reshape(layers, width // groups)

    joined_input = call(
        functools.partial(place_kernel, groups, capacity),
        "place_joined",
        [anywhere],
        shape((slots, width), bf16),
        hbm,
        [pltpu.VMEM((count, rows, packed), bf16), pltpu.VMEM((count, slots, GROUP), bf16), dma((count,)), dma((count,))],
        4 * slots * width,
        2 * rows * slots * width * 2,
    )(join_got)
    return (joined_input, soft_labels, log_partition[:, 0], gain_grad)


def solution(mesh):
    placed = (
        P(("group", "dp"), None),
        P(),
        P(("group", "dp"), None),
        P(("group", "dp"), None),
        P(("group", "dp"), None),
    )
    return jax.shard_map(
        per_device,
        mesh=mesh,
        in_specs=placed,
        out_specs=(
            P(("group", "dp"), None),
            P(("group", "dp"), None),
            P(("group", "dp")),
            P("group", "dp"),
        ),
        check_vma=False,
    )
```

```python
import functools

import jax
import jax.numpy as jnp
from jax import lax
from jax.experimental import pallas as pl
from jax.experimental.pallas import tpu as pltpu
from jax.sharding import PartitionSpec as P

eps = 1e-06
SUB = 8
GROUP = 2048
LANES = 128
PLANE = 4
CHUNKS = (2, 2)
VMEM_LIMIT = 20 * 1024 * 1024
VMEM_WHOLE = 56 * 1024 * 1024


def pieces_of(capacity):
    found, first = [], 0
    for size in (8, 4, 2, 1):
        while capacity - first >= size:
            found.append((first, size, SUB // size))
            first += size
    return found


def radices(size):
    found = []
    while size > 1:
        found.append(4 if size % 4 == 0 else 2)
        size //= found[-1]
    return found


def exchange_order(size):
    order = []
    for device in range(size):
        row, rest = 0, device
        for radix in radices(size):
            row, rest = row * radix + rest % radix, rest // radix
        order.append(row)
    return order


def iota(shape, dim):
    return lax.broadcasted_iota(jnp.int32, shape, dim)


def ranks_of(dest_row):
    tokens = dest_row.shape[1]
    across = jnp.broadcast_to(dest_row.astype(jnp.float32), (tokens, tokens))
    down = across.T
    same = across == down
    row, col = iota((tokens, tokens), 0), iota((tokens, tokens), 1)
    rank_row = jnp.sum(jnp.where(same & (row < col), 1.0, 0.0), axis=0, keepdims=True).astype(jnp.int32)
    rank_col = jnp.sum(jnp.where(same & (col < row), 1.0, 0.0), axis=1, keepdims=True).astype(jnp.int32)
    return dest_row, rank_row, down[:, :1].astype(jnp.int32), rank_col


def spread(target, rank, first, size, h):
    inside = (rank >= first) & (rank < first + size)
    return jnp.where(inside, target * SUB + h * size + rank - first, -1)


def hot(cond):
    return jnp.where(cond, 1.0, 0.0).astype(jnp.bfloat16)


def select(matrix, values):
    return jnp.dot(matrix, values, preferred_element_type=jnp.float32).astype(jnp.bfloat16)


def pack_matrices(target, rank, groups, capacity):
    shape = (groups * SUB, target.shape[1])
    out = []
    for first, size, splits in pieces_of(capacity):
        parts = [hot(iota(shape, 0) == spread(target, rank, first, size, h)) for h in range(splits)]
        out.append(parts[0] if splits == 1 else jnp.concatenate(parts, axis=1))
    return out


def pack_group(values, matrices, capacity):
    out = []
    for (_, _, splits), matrix in zip(pieces_of(capacity), matrices):
        wide = values.shape[1] // splits
        stacked = values if splits == 1 else jnp.concatenate([values[:, h * wide : (h + 1) * wide] for h in range(splits)], axis=0)
        out.append(select(matrix, stacked))
    return out


def unpack_matrices(target, rank, groups, capacity):
    shape = (target.shape[0], groups * SUB)
    runs = pieces_of(capacity)
    finest = max(splits for _, _, splits in runs)
    out = []
    for b in range(finest):
        parts = [hot(iota(shape, 1) == spread(target, rank, first, size, b * splits // finest)) for first, size, splits in runs]
        out.append(jnp.concatenate(parts, axis=1))
    return out


def unpack_group(packed, matrices, capacity, group):
    runs = pieces_of(capacity)
    finest = max(splits for _, _, splits in runs)
    wide = group // finest
    out = []
    for b in range(finest):
        parts, base = [], 0
        for _, _, splits in runs:
            own = group // splits
            at = base + b * wide - (b * splits // finest) * own
            parts.append(packed[:, at : at + wide])
            base += own
        out.append(jnp.dot(matrices[b], jnp.concatenate(parts, axis=0), preferred_element_type=jnp.float32))
    return out


def cols(ref, g, wide):
    return ref.at[:, g * wide : (g + 1) * wide]


def cot_kernel(
    groups, capacity, dest_hbm, logit_hbm, cot_hbm, out_hbm, dest_v, logit_v, cot_v, out_v, log_v, dest_sem, logit_sem, in_sem, out_sem, log_sem
):
    count, slots, group = cot_v.shape
    packed = out_v.shape[2]
    loads = [pltpu.make_async_copy(cols(cot_hbm, g, group), cot_v.at[g], in_sem.at[g]) for g in range(count)]
    stores = [pltpu.make_async_copy(out_v.at[g], cols(out_hbm, g, packed), out_sem.at[g]) for g in range(count)]
    dest_load = pltpu.make_async_copy(dest_hbm, dest_v, dest_sem)
    logit_load = pltpu.make_async_copy(logit_hbm, logit_v, logit_sem)
    dest_load.start()
    logit_load.start()
    for load in loads:
        load.start()
    dest_load.wait()
    target, rank, _, _ = ranks_of(dest_v[...])
    shape = (groups * SUB, target.shape[1])
    logit_load.wait()
    for m in range(log_v.shape[1] // LANES):
        place = hot(iota(shape, 0) == spread(target, rank, m * SUB, SUB, 0))
        log_v[:, m * LANES : (m + 1) * LANES] = select(place, logit_v[...])
    log_store = pltpu.make_async_copy(log_v, out_hbm.at[:, count * packed : count * packed + log_v.shape[1]], log_sem)
    log_store.start()
    slot = iota((1, slots), 1)
    matrices = pack_matrices(slot // capacity, slot % capacity, groups, capacity)
    for g in range(count):
        loads[g].wait()
        base = 0
        for block in pack_group(cot_v[g], matrices, capacity):
            out_v[g, :, base : base + block.shape[1]] = block
            base += block.shape[1]
        stores[g].start()
    for store in stores:
        store.wait()
    log_store.wait()


def place_of():
    me = lax.axis_index("dp")
    return lax.div(me, PLANE), lax.rem(me, PLANE)


def chunk_starts():
    first = 0
    for chunk, held in enumerate(CHUNKS):
        yield chunk, first, held
        first += held


def join_kernel(groups, capacity, dest_ref, gain_ref, feat_hbm, *refs):
    *outs, inv_ref, feat_v, out_v, in_sem, out_sem = refs
    layers, count, tokens, group = feat_v.shape
    width = count * group
    packed = out_v.shape[2]
    part = out_v.shape[1] // PLANE
    loads = [
        [pltpu.make_async_copy(cols(feat_hbm, l * count + g, group), feat_v.at[l, g], in_sem.at[l, g]) for g in range(count)]
        for l in range(layers)
    ]
    stores = []
    for chunk, first, held in chunk_starts():
        for g in range(held):
            stores.append(
                [
                    pltpu.make_async_copy(
                        out_v.at[first + g, q * part : (q + 1) * part], cols(outs[chunk * PLANE + q], g, packed), out_sem.at[first + g, q]
                    )
                    for q in range(PLANE)
                ]
            )
    for row in loads:
        for load in row:
            load.start()
    target, rank, _, _ = ranks_of(dest_ref[...])
    plane, within = place_of()
    target = (lax.rem(target, PLANE) ^ within) * (groups // PLANE) + (lax.div(target, PLANE) ^ plane)
    matrices = pack_matrices(target, rank, groups, capacity)
    lane = iota((tokens, LANES), 1)
    inv_all = jnp.zeros((tokens, LANES), jnp.float32)
    inverse = []
    for l in range(layers):
        total = jnp.zeros((tokens, LANES), jnp.float32)
        for g in range(count):
            loads[l][g].wait()
            for k in range(group // LANES):
                x = feat_v[l, g, :, k * LANES : (k + 1) * LANES].astype(jnp.float32)
                total = total + x * x
        mean = jnp.sum(total, axis=1, keepdims=True) / width
        inv = lax.rsqrt(mean + eps)
        inverse.append(inv)
        inv_all = jnp.where(lane == l, inv, inv_all)
    inv_ref[...] = inv_all
    for g in range(count):
        joined = None
        for l in range(layers):
            term = feat_v[l, g].astype(jnp.float32) * inverse[l] * gain_ref[l : l + 1, g * group : (g + 1) * group]
            joined = term if joined is None else joined + term
        base = 0
        for block in pack_group(joined.astype(jnp.bfloat16), matrices, capacity):
            out_v[g, :, base : base + block.shape[1]] = block
            base += block.shape[1]
        for store in stores[g]:
            store.start()
    for row in stores:
        for store in row:
            store.wait()


def grad_kernel(
    groups, capacity, dest_ref, inv_ref, feat_hbm, got_hbm, grad_ref, soft_ref, part_ref, feat_v, got_v, log_v, in_sem, got_sem, log_sem
):
    layers, count, tokens, group = feat_v.shape
    packed = got_v.shape[2]
    own = grad_ref.shape[1] // layers
    order = exchange_order(groups)
    log_load = pltpu.make_async_copy(got_hbm.at[:, count * packed : count * packed + log_v.shape[1]], log_v, log_sem)
    log_load.start()
    gots = [pltpu.make_async_copy(cols(got_hbm, g, packed), got_v.at[g], got_sem.at[g]) for g in range(count)]
    loads = [
        [pltpu.make_async_copy(cols(feat_hbm, l * count + g, group), feat_v.at[l, g], in_sem.at[l, g]) for g in range(count)]
        for l in range(layers)
    ]
    for g in range(count):
        gots[g].start()
        for l in range(layers):
            loads[l][g].start()
    _, _, target, rank = ranks_of(dest_ref[...])
    matrices = unpack_matrices(target, rank, groups, capacity)
    for g in range(count):
        gots[g].wait()
        for l in range(layers):
            loads[l][g].wait()
        blocks = unpack_group(got_v[g], matrices, capacity, group)
        wide = group // len(blocks)
        for b, cot in enumerate(blocks):
            step = min(own, wide)
            for l in range(layers):
                x = feat_v[l, g, :, b * wide : (b + 1) * wide].astype(jnp.float32)
                part = jnp.sum(x * inv_ref[:, l : l + 1] * cot, axis=0, keepdims=True)
                for u in range(wide // step):
                    at = g * group + b * wide + u * step
                    lo = l * own + at % own
                    row = order[at // own]
                    grad_ref[row : row + 1, lo : lo + step] = part[:, u * step : (u + 1) * step]
    log_load.wait()
    slots = soft_ref.shape[0]
    slot = iota((slots, 1), 0)
    target, rank = slot // capacity, slot % capacity
    shape = (slots, groups * SUB)
    logits = jnp.zeros((slots, LANES), jnp.float32)
    for m in range(log_v.shape[1] // LANES):
        place = hot(iota(shape, 1) == spread(target, rank, m * SUB, SUB, 0))
        logits = logits + jnp.dot(place, log_v[:, m * LANES : (m + 1) * LANES], preferred_element_type=jnp.float32)
    top = jnp.max(logits, axis=1, keepdims=True)
    partition = top + jnp.log(jnp.sum(jnp.exp(logits - top), axis=1, keepdims=True))
    part_ref[...] = partition
    soft_ref[...] = jnp.exp(logits - partition).astype(jnp.bfloat16)


def place_kernel(groups, capacity, first, *refs):
    planes = groups // PLANE
    gots, (out_hbm, got_v, out_v, in_sem, out_sem) = refs[:planes], refs[-5:]
    count, slots, group = out_v.shape
    packed = got_v.shape[2]
    part = got_v.shape[1] // planes
    loads = [
        [pltpu.make_async_copy(cols(got, g, packed), got_v.at[g, j * part : (j + 1) * part], in_sem.at[g, j]) for j, got in enumerate(gots)]
        for g in range(count)
    ]
    stores = [pltpu.make_async_copy(out_v.at[g], cols(out_hbm, first + g, group), out_sem.at[g]) for g in range(count)]
    for row in loads:
        for load in row:
            load.start()
    slot = iota((slots, 1), 0)
    plane, within = place_of()
    source, rank = lax.div(slot, capacity), lax.rem(slot, capacity)
    source = (lax.div(source, PLANE) ^ plane) * PLANE + (lax.rem(source, PLANE) ^ within)
    matrices = unpack_matrices(source, rank, groups, capacity)
    for g in range(count):
        for load in loads[g]:
            load.wait()
        blocks = unpack_group(got_v[g], matrices, capacity, group)
        wide = group // len(blocks)
        for b, block in enumerate(blocks):
            out_v[g, :, b * wide : (b + 1) * wide] = block.astype(jnp.bfloat16)
        stores[g].start()
    for store in stores:
        store.wait()


vmem = pl.BlockSpec(memory_space=pltpu.VMEM)
hbm = pl.BlockSpec(memory_space=pltpu.HBM)
anywhere = pl.BlockSpec(memory_space=pl.ANY)


def call(kernel, name, ins, out_shape, outs, scratch, moved, flops, limit=VMEM_LIMIT, aliases=None):
    return pl.pallas_call(
        kernel,
        out_shape=out_shape,
        in_specs=ins,
        out_specs=outs,
        scratch_shapes=scratch,
        compiler_params=pltpu.CompilerParams(vmem_limit_bytes=limit),
        cost_estimate=pl.CostEstimate(flops=flops, bytes_accessed=moved, transcendentals=0),
        input_output_aliases=aliases or {},
        name=name,
    )


def swap(blocks, axis, stride):
    size = lax.axis_size(axis)
    return [blocks[0]] + [lax.ppermute(block, axis, [(i, i ^ (m * stride)) for i in range(size)]) for m, block in enumerate(blocks) if m]


def reduce_rows(rows, axis):
    size = lax.axis_size(axis)
    me = lax.axis_index(axis)
    stride = 1
    for radix in radices(size):
        part = rows.shape[0] // radix
        digit = lax.rem(lax.div(me, stride), radix)
        total = lax.dynamic_slice_in_dim(rows, digit * part, part, 0)
        got = []
        for m in range(1, radix):
            sent = lax.dynamic_slice_in_dim(rows, (digit ^ m) * part, part, 0)
            got.append(lax.ppermute(sent, axis, [(i, i ^ (m * stride)) for i in range(size)]))
        for value in got:
            total = total + value
        rows = total
        stride *= radix
    return rows


def per_device(features, joining_gains, destination, target_logits, joined_cotangent):
    groups = lax.axis_size("dp")
    slots, width = joined_cotangent.shape
    capacity = slots // groups
    layers = joining_gains.shape[0]
    tokens, kept = target_logits.shape
    count = width // GROUP
    packed = GROUP * capacity // SUB
    rows = groups * SUB
    log_wide = -(-capacity // SUB) * kept
    bf16, f32, dma = jnp.bfloat16, jnp.float32, pltpu.SemaphoreType.DMA
    shape = jax.ShapeDtypeStruct
    dest_row = destination.reshape(1, tokens)

    cot_send = call(
        functools.partial(cot_kernel, groups, capacity),
        "pack_cotangent",
        [hbm, hbm, hbm],
        shape((rows, count * packed + log_wide), bf16),
        hbm,
        [
            pltpu.VMEM((1, tokens), jnp.int32),
            pltpu.VMEM((tokens, kept), bf16),
            pltpu.VMEM((count, slots, GROUP), bf16),
            pltpu.VMEM((count, rows, packed), bf16),
            pltpu.VMEM((rows, log_wide), bf16),
            dma,
            dma,
            dma((count,)),
            dma((count,)),
            dma,
        ],
        4 * slots * width,
        2 * rows * slots * width * 2,
        VMEM_WHOLE,
    )(dest_row, target_logits, joined_cotangent)
    cot_got = lax.all_to_all(cot_send, "dp", split_axis=0, concat_axis=0, tiled=True)

    planes = groups // PLANE
    part = planes * SUB
    *join_send, inverse = call(
        functools.partial(join_kernel, groups, capacity),
        "join_layers",
        [vmem, vmem, hbm],
        tuple(shape((part, held * packed), bf16) for held in CHUNKS for _ in range(PLANE)) + (shape((tokens, LANES), f32),),
        (hbm,) * (len(CHUNKS) * PLANE) + (vmem,),
        [
            pltpu.VMEM((layers, count, tokens, GROUP), bf16),
            pltpu.VMEM((count, rows, packed), bf16),
            dma((layers, count)),
            dma((count, PLANE)),
        ],
        2 * layers * tokens * width + 2 * slots * width,
        2 * rows * tokens * width * 2,
    )(dest_row, joining_gains, features)
    join_got = []
    for chunk, _, _ in chunk_starts():
        plane_got = swap(join_send[chunk * PLANE : (chunk + 1) * PLANE], "dp", 1)
        mixed = [jnp.concatenate([got[j * SUB : (j + 1) * SUB] for got in plane_got], axis=0) for j in range(planes)]
        join_got.append(swap(mixed, "dp", PLANE))

    partial_rows, soft_labels, log_partition = call(
        functools.partial(grad_kernel, groups, capacity),
        "gain_partials",
        [vmem, vmem, hbm, anywhere],
        (shape((groups, layers * width // groups), f32), shape((slots, kept), bf16), shape((slots, 1), f32)),
        (vmem, vmem, vmem),
        [
            pltpu.VMEM((layers, count, tokens, GROUP), bf16),
            pltpu.VMEM((count, rows, packed), bf16),
            pltpu.VMEM((rows, log_wide), bf16),
            dma((layers, count)),
            dma((count,)),
            dma,
        ],
        2 * layers * tokens * width + 2 * slots * width,
        2 * rows * tokens * width * 2,
    )(dest_row, inverse, features, cot_got)
    gain_grad = reduce_rows(partial_rows, "dp").reshape(layers, width // groups)

    joined_input = ()
    for chunk, first, held in chunk_starts():
        joined_input = (
            call(
                functools.partial(place_kernel, groups, capacity, first),
                "place_joined",
                [anywhere] * (planes + len(joined_input)),
                shape((slots, width), bf16),
                hbm,
                [
                    pltpu.VMEM((held, rows, packed), bf16),
                    pltpu.VMEM((held, slots, GROUP), bf16),
                    dma((held, planes)),
                    dma((held,)),
                ],
                4 * slots * held * GROUP,
                2 * rows * slots * held * GROUP * 2,
                aliases={planes: 0} if joined_input else None,
            )(*join_got[chunk], *joined_input),
        )
    joined_input = joined_input[0]
    return (joined_input, soft_labels, log_partition[:, 0], gain_grad)


def solution(mesh):
    placed = (
        P(("group", "dp"), None),
        P(),
        P(("group", "dp"), None),
        P(("group", "dp"), None),
        P(("group", "dp"), None),
    )
    return jax.shard_map(
        per_device,
        mesh=mesh,
        in_specs=placed,
        out_specs=(
            P(("group", "dp"), None),
            P(("group", "dp"), None),
            P(("group", "dp")),
            P("group", "dp"),
        ),
        check_vma=False,
    )
```

```python
import functools

import jax
import jax.numpy as jnp
from jax import lax
from jax.experimental import pallas as pl
from jax.experimental.pallas import tpu as pltpu
from jax.sharding import PartitionSpec as P

eps = 1e-06
SUB = 8
GROUP = 2048
LANES = 128
QUARTERS = 4
CORES = 2
VMEM_LIMIT = 20 * 1024 * 1024
VMEM_WHOLE = 56 * 1024 * 1024


def pieces_of(capacity):
    found, first = [], 0
    for size in (8, 4, 2, 1):
        while capacity - first >= size:
            found.append((first, size, SUB // size))
            first += size
    return found


def radices(size):
    found = []
    while size > 1:
        found.append(4 if size % 4 == 0 else 2)
        size //= found[-1]
    return found


def exchange_order(size):
    order = []
    for device in range(size):
        row, rest = 0, device
        for radix in radices(size):
            row, rest = row * radix + rest % radix, rest // radix
        order.append(row)
    return order


def iota(shape, dim):
    return lax.broadcasted_iota(jnp.int32, shape, dim)


def ranks_of(dest_row):
    tokens = dest_row.shape[1]
    across = jnp.broadcast_to(dest_row.astype(jnp.float32), (tokens, tokens))
    down = across.T
    same = across == down
    row, col = iota((tokens, tokens), 0), iota((tokens, tokens), 1)
    rank_row = jnp.sum(jnp.where(same & (row < col), 1.0, 0.0), axis=0, keepdims=True).astype(jnp.int32)
    rank_col = jnp.sum(jnp.where(same & (col < row), 1.0, 0.0), axis=1, keepdims=True).astype(jnp.int32)
    return dest_row, rank_row, down[:, :1].astype(jnp.int32), rank_col


def spread(target, rank, first, size, h):
    inside = (rank >= first) & (rank < first + size)
    return jnp.where(inside, target * SUB + h * size + rank - first, -1)


def hot(cond):
    return jnp.where(cond, 1.0, 0.0).astype(jnp.bfloat16)


def select(matrix, values):
    return jnp.dot(matrix, values, preferred_element_type=jnp.float32).astype(jnp.bfloat16)


def pack_matrices(target, rank, groups, capacity):
    shape = (groups * SUB, target.shape[1])
    out = []
    for first, size, splits in pieces_of(capacity):
        parts = [hot(iota(shape, 0) == spread(target, rank, first, size, h)) for h in range(splits)]
        out.append(parts[0] if splits == 1 else jnp.concatenate(parts, axis=1))
    return out


def pack_group(values, matrices, capacity):
    out = []
    for (_, _, splits), matrix in zip(pieces_of(capacity), matrices):
        wide = values.shape[1] // splits
        stacked = values if splits == 1 else jnp.concatenate([values[:, h * wide : (h + 1) * wide] for h in range(splits)], axis=0)
        out.append(select(matrix, stacked))
    return out


def unpack_matrices(target, rank, groups, capacity):
    shape = (target.shape[0], groups * SUB)
    runs = pieces_of(capacity)
    finest = max(splits for _, _, splits in runs)
    out = []
    for b in range(finest):
        parts = [hot(iota(shape, 1) == spread(target, rank, first, size, b * splits // finest)) for first, size, splits in runs]
        out.append(jnp.concatenate(parts, axis=1))
    return out


def unpack_group(packed, matrices, capacity, group):
    runs = pieces_of(capacity)
    finest = max(splits for _, _, splits in runs)
    wide = group // finest
    out = []
    for b in range(finest):
        parts, base = [], 0
        for _, _, splits in runs:
            own = group // splits
            at = base + b * wide - (b * splits // finest) * own
            parts.append(packed[:, at : at + wide])
            base += own
        out.append(jnp.dot(matrices[b], jnp.concatenate(parts, axis=0), preferred_element_type=jnp.float32))
    return out


def cols(ref, g, wide):
    return ref.at[:, g * wide : (g + 1) * wide]


def cot_kernel(
    groups, capacity, dest_hbm, logit_hbm, cot_hbm, *refs
):
    out_hbm, dest_v, logit_v, cot_v, out_v, log_v, dest_sem, logit_sem, in_sem, out_sem, log_sem = refs
    count, slots, group = cot_v.shape
    packed = out_v.shape[2]
    loads = [pltpu.make_async_copy(cols(cot_hbm, g, group), cot_v.at[g], in_sem.at[g]) for g in range(count)]
    stores = [pltpu.make_async_copy(out_v.at[g], cols(out_hbm, g, packed), out_sem.at[g]) for g in range(count)]
    dest_load = pltpu.make_async_copy(dest_hbm, dest_v, dest_sem)
    logit_load = pltpu.make_async_copy(logit_hbm, logit_v, logit_sem)
    dest_load.start()
    logit_load.start()
    for load in loads:
        load.start()
    dest_load.wait()
    target, rank, _, _ = ranks_of(dest_v[...])
    shape = (groups * SUB, target.shape[1])
    logit_load.wait()
    for m in range(log_v.shape[1] // LANES):
        place = hot(iota(shape, 0) == spread(target, rank, m * SUB, SUB, 0))
        log_v[:, m * LANES : (m + 1) * LANES] = select(place, logit_v[...])
    log_store = pltpu.make_async_copy(log_v, out_hbm.at[:, count * packed : count * packed + log_v.shape[1]], log_sem)
    log_store.start()
    slot = iota((1, slots), 1)
    matrices = pack_matrices(lax.div(slot, capacity), lax.rem(slot, capacity), groups, capacity)
    for g in range(count):
        loads[g].wait()
        base = 0
        for packed_block in pack_group(cot_v[g], matrices, capacity):
            out_v[g, :, base : base + packed_block.shape[1]] = packed_block
            base += packed_block.shape[1]
        stores[g].start()
    for store in stores + [log_store]:
        store.wait()


def join_kernel(groups, capacity, dest_ref, gain_ref, feat_hbm, *refs):
    *outs, inv_ref, feat_v, out_v, in_sem, out_sem = refs
    layers, count, tokens, group = feat_v.shape
    width = count * group
    packed = out_v.shape[2]
    part = out_v.shape[1] // CORES
    loads = [
        [pltpu.make_async_copy(cols(feat_hbm, l * count + g, group), feat_v.at[l, g], in_sem.at[l, g]) for g in range(count)]
        for l in range(layers)
    ]
    stores = [
        [
            pltpu.make_async_copy(out_v.at[g, q * part : (q + 1) * part], cols(outs[q], g, packed), out_sem.at[g, q])
            for q in range(CORES)
        ]
        for g in range(count)
    ]
    for row in loads:
        for load in row:
            load.start()
    target, rank, _, _ = ranks_of(dest_ref[...])
    target = target ^ lax.axis_index("dp")
    target = lax.rem(target, CORES) * (groups // CORES) + lax.div(target, CORES)
    matrices = pack_matrices(target, rank, groups, capacity)
    lane = iota((tokens, LANES), 1)
    inv_all = jnp.zeros((tokens, LANES), jnp.float32)
    inverse = []
    for l in range(layers):
        total = jnp.zeros((tokens, LANES), jnp.float32)
        for g in range(count):
            loads[l][g].wait()
            for k in range(group // LANES):
                x = feat_v[l, g, :, k * LANES : (k + 1) * LANES].astype(jnp.float32)
                total = total + x * x
        mean = jnp.sum(total, axis=1, keepdims=True) / width
        inv = lax.rsqrt(mean + eps)
        inverse.append(inv)
        inv_all = jnp.where(lane == l, inv, inv_all)
    inv_ref[...] = inv_all
    for g in range(count):
        joined = None
        for l in range(layers):
            term = feat_v[l, g].astype(jnp.float32) * inverse[l] * gain_ref[l : l + 1, g * group : (g + 1) * group]
            joined = term if joined is None else joined + term
        base = 0
        for block in pack_group(joined.astype(jnp.bfloat16), matrices, capacity):
            out_v[g, :, base : base + block.shape[1]] = block
            base += block.shape[1]
        for store in stores[g]:
            store.start()
    for row in stores:
        for store in row:
            store.wait()


def sort_kernel(chips, held, *refs):
    gots, outs, (got_v, out_v, in_sem, out_sem) = refs[:CORES], refs[CORES:-4], refs[-4:]
    count, rows, packed = got_v.shape
    own, part = chips * SUB, CORES * SUB
    loads = [
        [pltpu.make_async_copy(cols(got, g, packed), got_v.at[g, q * own : (q + 1) * own], in_sem.at[g, q]) for q, got in enumerate(gots)]
        for g in range(count)
    ]
    stores = [
        [
            pltpu.make_async_copy(
                out_v.at[g, j * part : (j + 1) * part],
                outs[array].at[pl.ds(row, part), g * packed : (g + 1) * packed],
                out_sem.at[g, j],
            )
            for j, (array, row) in enumerate(held)
        ]
        for g in range(count)
    ]
    for row in loads:
        for load in row:
            load.start()
    at, come = iota((rows, rows), 0), iota((rows, rows), 1)
    chip, core, rank = lax.div(at, part), lax.rem(lax.div(at, SUB), CORES), lax.rem(at, SUB)
    matrix = hot(come == core * own + chip * SUB + rank)
    for g in range(count):
        for load in loads[g]:
            load.wait()
        out_v[g] = select(matrix, got_v[g])
        for store in stores[g]:
            store.start()
    for row in stores:
        for store in row:
            store.wait()


def grad_kernel(
    groups, capacity, dest_ref, inv_ref, feat_hbm, got_hbm, grad_ref, soft_ref, part_ref, feat_v, got_v, log_v, in_sem, got_sem, log_sem
):
    layers, count, tokens, group = feat_v.shape
    packed = got_v.shape[2]
    own = grad_ref.shape[2]
    order = exchange_order(groups)
    log_load = pltpu.make_async_copy(got_hbm.at[:, count * packed : count * packed + log_v.shape[1]], log_v, log_sem)
    log_load.start()
    gots = [pltpu.make_async_copy(cols(got_hbm, g, packed), got_v.at[g], got_sem.at[g]) for g in range(count)]
    loads = [
        [pltpu.make_async_copy(cols(feat_hbm, l * count + g, group), feat_v.at[l, g], in_sem.at[l, g]) for g in range(count)]
        for l in range(layers)
    ]
    for g in range(count):
        gots[g].start()
        for l in range(layers):
            loads[l][g].start()
    _, _, target, rank = ranks_of(dest_ref[...])
    matrices = unpack_matrices(target, rank, groups, capacity)
    for g in range(count):
        gots[g].wait()
        for l in range(layers):
            loads[l][g].wait()
        blocks = unpack_group(got_v[g], matrices, capacity, group)
        wide = group // len(blocks)
        for b, cot in enumerate(blocks):
            step = min(own, wide)
            for l in range(layers):
                x = feat_v[l, g, :, b * wide : (b + 1) * wide].astype(jnp.float32)
                part = jnp.sum(x * inv_ref[:, l : l + 1] * cot, axis=0, keepdims=True)
                for u in range(wide // step):
                    at = g * group + b * wide + u * step
                    lo = at % own
                    grad_ref[order[at // own], l : l + 1, lo : lo + step] = part[:, u * step : (u + 1) * step]
    log_load.wait()
    slots = soft_ref.shape[0]
    slot = iota((slots, 1), 0)
    target, rank = lax.div(slot, capacity), lax.rem(slot, capacity)
    shape = (slots, groups * SUB)
    logits = jnp.zeros((slots, LANES), jnp.float32)
    for m in range(log_v.shape[1] // LANES):
        place = hot(iota(shape, 1) == spread(target, rank, m * SUB, SUB, 0))
        logits = logits + jnp.dot(place, log_v[:, m * LANES : (m + 1) * LANES], preferred_element_type=jnp.float32)
    top = jnp.max(logits, axis=1, keepdims=True)
    partition = top + jnp.log(jnp.sum(jnp.exp(logits - top), axis=1, keepdims=True))
    part_ref[...] = jnp.broadcast_to(partition, logits.shape).T[:1]
    soft_ref[...] = jnp.exp(logits - partition).astype(jnp.bfloat16)


def place_kernel(groups, capacity, away, found, *refs):
    chips = groups // QUARTERS // CORES
    gots, (out_hbm, got_v, out_v, in_sem, out_sem) = refs[:-5], refs[-5:]
    _, count, held, group = out_v.shape
    packed = got_v.shape[3]
    part = CORES * SUB
    me = lax.axis_index("dp")
    quarter, within = lax.div(me, groups // QUARTERS), lax.rem(me, groups // QUARTERS)
    loads, stores = [], []
    for a, j in enumerate(away):
        rows = pl.ds(pl.multiple_of((quarter ^ j) * held, held), held)
        for g in range(count):
            loads.append(
                [
                    pltpu.make_async_copy(
                        gots[array].at[pl.ds(row, part), g * packed : (g + 1) * packed],
                        got_v.at[a, g, i * part : (i + 1) * part],
                        in_sem.at[a, g, i],
                    )
                    for i, (array, row) in enumerate(found[a * chips : (a + 1) * chips])
                ]
            )
            stores.append(pltpu.make_async_copy(out_v.at[a, g], out_hbm.at[rows, g * group : (g + 1) * group], out_sem.at[a, g]))
    for row in loads:
        for load in row:
            load.start()
    slot = iota((held, 1), 0)
    matrices = unpack_matrices(lax.div(slot, capacity) ^ within, lax.rem(slot, capacity), groups // QUARTERS, capacity)
    for a in range(len(away)):
        for g in range(count):
            for load in loads[a * count + g]:
                load.wait()
            blocks = unpack_group(got_v[a, g], matrices, capacity, group)
            wide = group // len(blocks)
            for b, block in enumerate(blocks):
                out_v[a, g, :, b * wide : (b + 1) * wide] = block.astype(jnp.bfloat16)
            stores[a * count + g].start()
    for store in stores:
        store.wait()


vmem = pl.BlockSpec(memory_space=pltpu.VMEM)
hbm = pl.BlockSpec(memory_space=pltpu.HBM)
anywhere = pl.BlockSpec(memory_space=pl.ANY)


def call(kernel, name, ins, out_shape, outs, scratch, moved, flops, limit=VMEM_LIMIT, aliases=None):
    return pl.pallas_call(
        kernel,
        out_shape=out_shape,
        in_specs=ins,
        out_specs=outs,
        scratch_shapes=scratch,
        compiler_params=pltpu.CompilerParams(vmem_limit_bytes=limit),
        cost_estimate=pl.CostEstimate(flops=flops, bytes_accessed=moved, transcendentals=0),
        input_output_aliases=aliases or {},
        name=name,
    )


def across(block, axis, bits):
    return lax.ppermute(block, axis, [(i, i ^ bits) for i in range(lax.axis_size(axis))])


def reduce_rows(rows, axis):
    size = lax.axis_size(axis)
    me = lax.axis_index(axis)
    stride = 1
    for radix in radices(size):
        part = rows.shape[0] // radix
        digit = lax.rem(lax.div(me, stride), radix)
        total = lax.dynamic_slice_in_dim(rows, digit * part, part, 0)
        got = []
        for m in range(1, radix):
            sent = lax.dynamic_slice_in_dim(rows, (digit ^ m) * part, part, 0)
            got.append(lax.ppermute(sent, axis, [(i, i ^ (m * stride)) for i in range(size)]))
        for value in got:
            total = total + value
        rows = total
        stride *= radix
    return rows


def per_device(features, joining_gains, destination, target_logits, joined_cotangent):
    groups = lax.axis_size("dp")
    slots, width = joined_cotangent.shape
    capacity = slots // groups
    layers = joining_gains.shape[0]
    tokens, kept = target_logits.shape
    count = width // GROUP
    packed = GROUP * capacity // SUB
    rows = groups * SUB
    log_wide = -(-capacity // SUB) * kept
    bf16, f32, dma = jnp.bfloat16, jnp.float32, pltpu.SemaphoreType.DMA
    shape = jax.ShapeDtypeStruct
    dest_row = destination.reshape(1, tokens)

    chips = groups // CORES
    near = chips // QUARTERS

    cot_send = call(
        functools.partial(cot_kernel, groups, capacity),
        "pack_cotangent",
        [hbm, hbm, hbm],
        shape((rows, count * packed + log_wide), bf16),
        hbm,
        [
            pltpu.VMEM((1, tokens), jnp.int32),
            pltpu.VMEM((tokens, kept), bf16),
            pltpu.VMEM((count, slots, GROUP), bf16),
            pltpu.VMEM((count, rows, packed), bf16),
            pltpu.VMEM((rows, log_wide), bf16),
            dma,
            dma,
            dma((count,)),
            dma((count,)),
            dma,
        ],
        4 * slots * width,
        2 * rows * slots * width * 2,
        VMEM_WHOLE,
    )(dest_row, target_logits, joined_cotangent)

    cot_got = lax.all_to_all(cot_send, "dp", split_axis=0, concat_axis=0, tiled=True)

    *join_send, inverse = call(
        functools.partial(join_kernel, groups, capacity),
        "join_layers",
        [vmem, vmem, hbm],
        (shape((chips * SUB, count * packed), bf16),) * CORES + (shape((tokens, LANES), f32),),
        (hbm,) * CORES + (vmem,),
        [
            pltpu.VMEM((layers, count, tokens, GROUP), bf16),
            pltpu.VMEM((count, rows, packed), bf16),
            dma((layers, count)),
            dma((count, CORES)),
        ],
        2 * layers * tokens * width + 2 * slots * width,
        2 * rows * tokens * width * 2,
    )(dest_row, joining_gains, features)
    part = CORES * SUB
    relayed = near == 2
    held = [(0, 0), (1, 0), (2, 0), (1, part)] if relayed else []
    held += [(k - 1 if relayed else k, 0) for k in range(len(held), chips)]
    tall = [sum(part for array, _ in held if array == i) for i in range(1 + held[-1][0])]
    join_sorted = call(
        functools.partial(sort_kernel, chips, held),
        "sort_chips",
        [anywhere] * CORES,
        tuple(shape((size, count * packed), bf16) for size in tall),
        (hbm,) * len(tall),
        [
            pltpu.VMEM((count, rows, packed), bf16),
            pltpu.VMEM((count, rows, packed), bf16),
            dma((count, CORES)),
            dma((count, chips)),
        ],
        4 * slots * width,
        2 * rows * rows * width,
    )(join_send[0], across(join_send[1], "dp", 1))
    if relayed:
        first = across(join_sorted[1], "dp", CORES)
        second = across(jnp.concatenate([join_sorted[2], first[part:]], axis=0), "dp", 2 * CORES)
        join_got = [(join_sorted[0], 0), (first, 0), (second, 0), (second, part)]
    else:
        join_got = [(join_sorted[0], 0)]
    for k in range(len(join_got), chips):
        join_got.append((across(join_sorted[held[k][0]], "dp", k * CORES), 0))

    partial_rows, soft_labels, log_partition = call(
        functools.partial(grad_kernel, groups, capacity),
        "gain_partials",
        [vmem, vmem, hbm, anywhere],
        (shape((groups, layers, width // groups), f32), shape((slots, kept), bf16), shape((1, slots), f32)),
        (vmem, vmem, vmem),
        [
            pltpu.VMEM((layers, count, tokens, GROUP), bf16),
            pltpu.VMEM((count, rows, packed), bf16),
            pltpu.VMEM((rows, log_wide), bf16),
            dma((layers, count)),
            dma((count,)),
            dma,
        ],
        2 * layers * tokens * width + 2 * slots * width,
        2 * rows * tokens * width * 2,
    )(dest_row, inverse, features, cot_got)
    gain_grad = reduce_rows(partial_rows, "dp")[0]

    joined_input = ()
    for away in ((0, 1), (2,), (3,)):
        parts = [join_got[j * near + i] for j in away for i in range(near)]
        arrays = []
        for array, _ in parts:
            if not any(array is seen for seen in arrays):
                arrays.append(array)
        found = [([array is seen for seen in arrays].index(True), row) for array, row in parts]
        joined_input = (
            call(
                functools.partial(place_kernel, groups, capacity, away, found),
                "place_joined",
                [anywhere] * (len(arrays) + len(joined_input)),
                shape((slots, width), bf16),
                hbm,
                [
                    pltpu.VMEM((len(away), count, rows // QUARTERS, packed), bf16),
                    pltpu.VMEM((len(away), count, slots // QUARTERS, GROUP), bf16),
                    dma((len(away), count, near)),
                    dma((len(away), count)),
                ],
                slots * width * len(away),
                rows * slots * width * len(away),
                aliases={len(arrays): 0} if joined_input else None,
            )(*arrays, *joined_input),
        )
    joined_input = joined_input[0]
    return (joined_input, soft_labels, log_partition[0], gain_grad)


def solution(mesh):
    placed = (
        P(("group", "dp"), None),
        P(),
        P(("group", "dp"), None),
        P(("group", "dp"), None),
        P(("group", "dp"), None),
    )
    return jax.shard_map(
        per_device,
        mesh=mesh,
        in_specs=placed,
        out_specs=(
            P(("group", "dp"), None),
            P(("group", "dp"), None),
            P(("group", "dp")),
            P("group", "dp"),
        ),
        check_vma=False,
    )
```

```python
import functools

import jax
import jax.numpy as jnp
from jax import lax
from jax.experimental import pallas as pl
from jax.experimental.pallas import tpu as pltpu
from jax.sharding import PartitionSpec as P

eps = 1e-06
SUB = 8
GROUP = 2048
LANES = 128
QUARTERS = 4
CORES = 2
VMEM_LIMIT = 24 * 1024 * 1024


def pieces_of(capacity):
    found, first = [], 0
    for size in (8, 4, 2, 1):
        while capacity - first >= size:
            found.append((first, size, SUB // size))
            first += size
    return found


def radices(size):
    found = []
    while size > 1:
        found.append(4 if size % 4 == 0 else 2)
        size //= found[-1]
    return found


def exchange_order(size):
    order = []
    for device in range(size):
        row, rest = 0, device
        for radix in radices(size):
            row, rest = row * radix + rest % radix, rest // radix
        order.append(row)
    return order


def iota(shape, dim):
    return lax.broadcasted_iota(jnp.int32, shape, dim)


def ranks_of(dest_row):
    tokens = dest_row.shape[1]
    across = jnp.broadcast_to(dest_row.astype(jnp.float32), (tokens, tokens))
    down = across.T
    same = across == down
    row, col = iota((tokens, tokens), 0), iota((tokens, tokens), 1)
    rank_row = jnp.sum(jnp.where(same & (row < col), 1.0, 0.0), axis=0, keepdims=True).astype(jnp.int32)
    rank_col = jnp.sum(jnp.where(same & (col < row), 1.0, 0.0), axis=1, keepdims=True).astype(jnp.int32)
    return dest_row, rank_row, down[:, :1].astype(jnp.int32), rank_col


def spread(target, rank, first, size, h):
    inside = (rank >= first) & (rank < first + size)
    return jnp.where(inside, target * SUB + h * size + rank - first, -1)


def hot(cond):
    return jnp.where(cond, 1.0, 0.0).astype(jnp.bfloat16)


def select(matrix, values):
    return jnp.dot(matrix, values, preferred_element_type=jnp.float32).astype(jnp.bfloat16)


def pack_matrices(target, rank, groups, capacity):
    shape = (groups * SUB, target.shape[1])
    out = []
    for first, size, splits in pieces_of(capacity):
        parts = [hot(iota(shape, 0) == spread(target, rank, first, size, h)) for h in range(splits)]
        out.append(parts[0] if splits == 1 else jnp.concatenate(parts, axis=1))
    return out


def pack_group(values, matrices, capacity):
    out = []
    for (_, _, splits), matrix in zip(pieces_of(capacity), matrices):
        wide = values.shape[1] // splits
        stacked = values if splits == 1 else jnp.concatenate([values[:, h * wide : (h + 1) * wide] for h in range(splits)], axis=0)
        out.append(select(matrix, stacked))
    return out


def unpack_matrices(target, rank, groups, capacity):
    shape = (target.shape[0], groups * SUB)
    runs = pieces_of(capacity)
    finest = max(splits for _, _, splits in runs)
    out = []
    for b in range(finest):
        parts = [hot(iota(shape, 1) == spread(target, rank, first, size, b * splits // finest)) for first, size, splits in runs]
        out.append(jnp.concatenate(parts, axis=1))
    return out


def unpack_group(packed, matrices, capacity, group):
    runs = pieces_of(capacity)
    finest = max(splits for _, _, splits in runs)
    wide = group // finest
    out = []
    for b in range(finest):
        parts, base = [], 0
        for _, _, splits in runs:
            own = group // splits
            at = base + b * wide - (b * splits // finest) * own
            parts.append(packed[:, at : at + wide])
            base += own
        out.append(jnp.dot(matrices[b], jnp.concatenate(parts, axis=0), preferred_element_type=jnp.float32))
    return out


def cols(ref, g, wide):
    return ref.at[:, g * wide : (g + 1) * wide]


def join_kernel(groups, capacity, dest_ref, logit_ref, gain_ref, feat_hbm, *refs):
    *outs, share_hbm, inv_ref, share_inv_ref, feat_v, out_v, log_v, share_v, in_sem, out_sem, log_sem, share_sem = refs
    layers, count, tokens, group = feat_v.shape
    width = count * group
    packed = out_v.shape[2]
    part = out_v.shape[1] // CORES
    loads = [
        [pltpu.make_async_copy(cols(feat_hbm, l * count + g, group), feat_v.at[l, g], in_sem.at[l, g]) for g in range(count)]
        for l in range(layers)
    ]
    stores = [
        [
            pltpu.make_async_copy(out_v.at[g, q * part : (q + 1) * part], cols(outs[q], g, packed), out_sem.at[g, q])
            for q in range(CORES)
        ]
        for g in range(count)
    ]
    for row in loads:
        for load in row:
            load.start()
    target, rank, _, _ = ranks_of(dest_ref[...])
    me = lax.axis_index("dp")
    own = share_hbm.shape[0]
    given = jnp.where(lax.rem(target, CORES) == lax.rem(me, CORES), -1, lax.div(target, CORES) * capacity + rank)
    shared = iota((own, tokens), 0) == given
    shares = [
        [pltpu.make_async_copy(share_v.at[l, g], cols(share_hbm, l * count + g, group), share_sem.at[l, g]) for g in range(count)]
        for l in range(layers)
    ]
    target = target ^ me
    target = lax.rem(target, CORES) * (groups // CORES) + lax.div(target, CORES)
    shape = (groups * SUB, tokens)
    for m in range(log_v.shape[1] // LANES):
        place = hot(iota(shape, 0) == spread(target, rank, m * SUB, SUB, 0))
        log_v[:, m * LANES : (m + 1) * LANES] = select(place, logit_ref[...])
    tail = slice(count * packed, count * packed + log_v.shape[1])
    stores.append([pltpu.make_async_copy(log_v.at[q * part : (q + 1) * part], outs[q].at[:, tail], log_sem.at[q]) for q in range(CORES)])
    for store in stores[-1]:
        store.start()
    matrices = pack_matrices(target, rank, groups, capacity)
    lane = iota((tokens, LANES), 1)
    inv_all = jnp.zeros((tokens, LANES), jnp.float32)
    inverse = []
    for l in range(layers):
        total = jnp.zeros((tokens, LANES), jnp.float32)
        for g in range(count):
            loads[l][g].wait()
            for k in range(group // LANES):
                x = feat_v[l, g, :, k * LANES : (k + 1) * LANES].astype(jnp.float32)
                total = total + x * x
        mean = jnp.sum(total, axis=1, keepdims=True) / width
        inv = lax.rsqrt(mean + eps)
        inverse.append(inv)
        inv_all = jnp.where(lane == l, inv, inv_all)
    inv_ref[...] = inv_all
    share_inv_ref[...] = jnp.dot(
        jnp.where(shared, 1.0, 0.0), inv_all, preferred_element_type=jnp.float32, precision=lax.Precision.HIGHEST
    )
    for g in range(count):
        joined = None
        for l in range(layers):
            term = feat_v[l, g].astype(jnp.float32) * inverse[l] * gain_ref[l : l + 1, g * group : (g + 1) * group]
            joined = term if joined is None else joined + term
        base = 0
        for block in pack_group(joined.astype(jnp.bfloat16), matrices, capacity):
            out_v[g, :, base : base + block.shape[1]] = block
            base += block.shape[1]
        for store in stores[g]:
            store.start()
    for l in range(layers):
        for g in range(count):
            share_v[l, g] = select(hot(shared), feat_v[l, g])
            shares[l][g].start()
    for row in stores + shares:
        for store in row:
            store.wait()


def sort_kernel(chips, held, widths, *refs):
    gots, outs, (got_v, out_v, in_sem, out_sem) = refs[:CORES], refs[CORES:-4], refs[-4:]
    rows = got_v.shape[1]
    own, part = chips * SUB, CORES * SUB
    loads, stores, base = [], [], 0
    for g, wide in enumerate(widths):
        span = slice(base, base + wide)
        base += wide
        loads.append(
            [
                pltpu.make_async_copy(got.at[:, span], got_v.at[g, q * own : (q + 1) * own, :wide], in_sem.at[g, q])
                for q, got in enumerate(gots)
            ]
        )
        stores.append(
            [
                pltpu.make_async_copy(out_v.at[g, j * part : (j + 1) * part, :wide], outs[array].at[pl.ds(row, part), span], out_sem.at[g, j])
                for j, (array, row) in enumerate(held)
            ]
        )
    for row in loads:
        for load in row:
            load.start()
    at, come = iota((rows, rows), 0), iota((rows, rows), 1)
    chip, core, rank = lax.div(at, part), lax.rem(lax.div(at, SUB), CORES), lax.rem(at, SUB)
    matrix = hot(come == core * own + chip * SUB + rank)
    for g, wide in enumerate(widths):
        for load in loads[g]:
            load.wait()
        out_v[g, :, :wide] = select(matrix, got_v[g, :, :wide])
        for store in stores[g]:
            store.start()
    for row in stores:
        for store in row:
            store.wait()


def grad_kernel(
    groups, capacity, dest_ref, inv_ref, feat_hbm, other_inv_ref, other_hbm, got_hbm, grad_ref, feat_v, got_v, in_sem, other_sem, got_sem
):
    layers, count, both, group = feat_v.shape
    tokens = inv_ref.shape[0]
    slots = got_v.shape[1]
    own = grad_ref.shape[2]
    order = exchange_order(groups)
    gots = [pltpu.make_async_copy(cols(got_hbm, g, group), got_v.at[g], got_sem.at[g]) for g in range(count)]
    loads = [
        [
            (
                pltpu.make_async_copy(cols(feat_hbm, l * count + g, group), feat_v.at[l, g, :tokens], in_sem.at[l, g]),
                pltpu.make_async_copy(cols(other_hbm, l * count + g, group), feat_v.at[l, g, tokens:both], other_sem.at[l, g]),
            )
            for g in range(count)
        ]
        for l in range(layers)
    ]
    for g in range(count):
        gots[g].start()
        for l in range(layers):
            for load in loads[l][g]:
                load.start()
    _, _, target, rank = ranks_of(dest_ref[...])
    mine = lax.rem(lax.axis_index("dp"), CORES)
    row = jnp.where(lax.rem(target, CORES) == mine, target * capacity + rank, -1)
    come = iota((both - tokens, 1), 0)
    come = (lax.div(come, capacity) * CORES + 1 - mine) * capacity + lax.rem(come, capacity)
    matrix = hot(iota((both, slots), 1) == jnp.concatenate([row, come], axis=0))
    inverse = jnp.concatenate([inv_ref[...], other_inv_ref[...]], axis=0)
    wide = group // 2
    step = min(own, wide)
    for g in range(count):
        gots[g].wait()
        for l in range(layers):
            for load in loads[l][g]:
                load.wait()
        for b in range(group // wide):
            cot = jnp.dot(matrix, got_v[g, :, b * wide : (b + 1) * wide], preferred_element_type=jnp.float32)
            for l in range(layers):
                x = feat_v[l, g, :, b * wide : (b + 1) * wide].astype(jnp.float32)
                part = jnp.sum(x * inverse[:, l : l + 1] * cot, axis=0, keepdims=True)
                for u in range(wide // step):
                    at = g * group + b * wide + u * step
                    lo = at % own
                    grad_ref[order[at // own], l : l + 1, lo : lo + step] = part[:, u * step : (u + 1) * step]


def place_kernel(groups, capacity, away, found, logs, *refs):
    chips = groups // QUARTERS // CORES
    part = CORES * SUB
    if logs:
        *gots, out_hbm, soft_ref, part_ref, got_v, out_v, in_sem, out_sem, log_v, log_sem = refs
    else:
        *gots, out_hbm, got_v, out_v, in_sem, out_sem = refs
    _, count, held, group = out_v.shape
    packed = got_v.shape[3]
    me = lax.axis_index("dp")
    quarter, within = lax.div(me, groups // QUARTERS), lax.rem(me, groups // QUARTERS)
    loads, stores = [], []
    for a, j in enumerate(away):
        rows = pl.ds(pl.multiple_of((quarter ^ j) * held, held), held)
        for g in range(count):
            loads.append(
                [
                    pltpu.make_async_copy(
                        gots[array].at[pl.ds(row, part), g * packed : (g + 1) * packed],
                        got_v.at[a, g, i * part : (i + 1) * part],
                        in_sem.at[a, g, i],
                    )
                    for i, (array, row) in enumerate(found[a * chips : (a + 1) * chips])
                ]
            )
            stores.append(pltpu.make_async_copy(out_v.at[a, g], out_hbm.at[rows, g * group : (g + 1) * group], out_sem.at[a, g]))
    log_loads = []
    for k, (array, row) in enumerate(logs):
        span = slice(count * packed, count * packed + log_v.shape[1])
        log_loads.append(pltpu.make_async_copy(gots[array].at[pl.ds(row, part), span], log_v.at[k * part : (k + 1) * part], log_sem.at[k]))
    for row in loads + [log_loads]:
        for load in row:
            load.start()
    slot = iota((held, 1), 0)
    matrices = unpack_matrices(lax.div(slot, capacity) ^ within, lax.rem(slot, capacity), groups // QUARTERS, capacity)
    for a in range(len(away)):
        for g in range(count):
            for load in loads[a * count + g]:
                load.wait()
            blocks = unpack_group(got_v[a, g], matrices, capacity, group)
            wide = group // len(blocks)
            for b, block in enumerate(blocks):
                out_v[a, g, :, b * wide : (b + 1) * wide] = block.astype(jnp.bfloat16)
            stores[a * count + g].start()
    if logs:
        for load in log_loads:
            load.wait()
        slots = soft_ref.shape[0]
        slot = iota((slots, 1), 0)
        source, rank = lax.div(slot, capacity) ^ me, lax.rem(slot, capacity)
        shape = (slots, groups * SUB)
        logits = jnp.zeros((slots, LANES), jnp.float32)
        for m in range(log_v.shape[1] // LANES):
            place = hot(iota(shape, 1) == spread(source, rank, m * SUB, SUB, 0))
            logits = logits + jnp.dot(place, log_v[:, m * LANES : (m + 1) * LANES], preferred_element_type=jnp.float32)
        top = jnp.max(logits, axis=1, keepdims=True)
        partition = top + jnp.log(jnp.sum(jnp.exp(logits - top), axis=1, keepdims=True))
        part_ref[...] = jnp.broadcast_to(partition, logits.shape).T[:1]
        soft_ref[...] = jnp.exp(logits - partition).astype(jnp.bfloat16)
    for store in stores:
        store.wait()


vmem = pl.BlockSpec(memory_space=pltpu.VMEM)
hbm = pl.BlockSpec(memory_space=pltpu.HBM)
anywhere = pl.BlockSpec(memory_space=pl.ANY)


def call(kernel, name, ins, out_shape, outs, scratch, moved, flops, limit=VMEM_LIMIT, aliases=None):
    return pl.pallas_call(
        kernel,
        out_shape=out_shape,
        in_specs=ins,
        out_specs=outs,
        scratch_shapes=scratch,
        compiler_params=pltpu.CompilerParams(vmem_limit_bytes=limit),
        cost_estimate=pl.CostEstimate(flops=flops, bytes_accessed=moved, transcendentals=0),
        input_output_aliases=aliases or {},
        name=name,
    )


def across(block, axis, bits):
    return lax.ppermute(block, axis, [(i, i ^ bits) for i in range(lax.axis_size(axis))])


def reduce_rows(rows, axis):
    size = lax.axis_size(axis)
    me = lax.axis_index(axis)
    stride = 1
    for radix in radices(size):
        part = rows.shape[0] // radix
        digit = lax.rem(lax.div(me, stride), radix)
        total = lax.dynamic_slice_in_dim(rows, digit * part, part, 0)
        got = []
        for m in range(1, radix):
            sent = lax.dynamic_slice_in_dim(rows, (digit ^ m) * part, part, 0)
            got.append(lax.ppermute(sent, axis, [(i, i ^ (m * stride)) for i in range(size)]))
        for value in got:
            total = total + value
        rows = total
        stride *= radix
    return rows


def per_device(features, joining_gains, destination, target_logits, joined_cotangent):
    groups = lax.axis_size("dp")
    slots, width = joined_cotangent.shape
    capacity = slots // groups
    layers = joining_gains.shape[0]
    tokens, kept = target_logits.shape
    count = width // GROUP
    packed = GROUP * capacity // SUB
    rows = groups * SUB
    log_wide = -(-capacity // SUB) * kept
    bf16, f32, dma = jnp.bfloat16, jnp.float32, pltpu.SemaphoreType.DMA
    shape = jax.ShapeDtypeStruct
    dest_row = destination.reshape(1, tokens)

    chips = groups // CORES
    near = chips // QUARTERS
    wide = count * packed + log_wide

    by_core = [[chip * CORES + core for chip in range(chips)] for core in range(CORES)]
    cot_chip = lax.all_to_all(joined_cotangent, "dp", split_axis=0, concat_axis=0, axis_index_groups=by_core, tiled=True)

    *join_send, share, inverse, share_inverse = call(
        functools.partial(join_kernel, groups, capacity),
        "join_layers",
        [vmem, vmem, vmem, hbm],
        (shape((chips * SUB, wide), bf16),) * CORES
        + (shape((slots // CORES, layers * width), bf16), shape((tokens, LANES), f32), shape((slots // CORES, LANES), f32)),
        (hbm,) * CORES + (hbm, vmem, vmem),
        [
            pltpu.VMEM((layers, count, tokens, GROUP), bf16),
            pltpu.VMEM((count, rows, packed), bf16),
            pltpu.VMEM((rows, log_wide), bf16),
            pltpu.VMEM((layers, count, slots // CORES, GROUP), bf16),
            dma((layers, count)),
            dma((count, CORES)),
            dma((CORES,)),
            dma((layers, count)),
        ],
        2 * layers * tokens * width + 2 * slots * width,
        2 * rows * tokens * width * 2,
    )(dest_row, target_logits, joining_gains, features)
    part = CORES * SUB
    relayed = near == 2
    held = [(0, 0), (1, 0), (2, 0), (1, part)] if relayed else []
    held += [(k - 1 if relayed else k, 0) for k in range(len(held), chips)]
    tall = [sum(part for array, _ in held if array == i) for i in range(1 + held[-1][0])]
    widths = (packed,) * count + (log_wide,)
    join_sorted = call(
        functools.partial(sort_kernel, chips, held, widths),
        "sort_chips",
        [anywhere] * CORES,
        tuple(shape((size, wide), bf16) for size in tall),
        (hbm,) * len(tall),
        [
            pltpu.VMEM((len(widths), rows, packed), bf16),
            pltpu.VMEM((len(widths), rows, packed), bf16),
            dma((len(widths), CORES)),
            dma((len(widths), chips)),
        ],
        4 * slots * width,
        2 * rows * rows * width,
    )(join_send[0], across(join_send[1], "dp", 1))
    if relayed:
        first = across(join_sorted[1], "dp", CORES)
        second = across(jnp.concatenate([join_sorted[2], first[part:]], axis=0), "dp", 2 * CORES)
        join_got = [(join_sorted[0], 0), (first, 0), (second, 0), (second, part)]
    else:
        join_got = [(join_sorted[0], 0)]
    for k in range(len(join_got), chips):
        join_got.append((across(join_sorted[held[k][0]], "dp", k * CORES), 0))

    partial_rows = call(
        functools.partial(grad_kernel, groups, capacity),
        "gain_partials",
        [vmem, vmem, hbm, vmem, anywhere, anywhere],
        shape((groups, layers, width // groups), f32),
        vmem,
        [
            pltpu.VMEM((layers, count, tokens + slots // CORES, GROUP), bf16),
            pltpu.VMEM((count, slots, GROUP), bf16),
            dma((layers, count)),
            dma((layers, count)),
            dma((count,)),
        ],
        2 * layers * tokens * width + 2 * slots * width,
        2 * rows * tokens * width * 2,
    )(dest_row, inverse, features, across(share_inverse, "dp", 1), across(share, "dp", 1), cot_chip)
    gain_grad = reduce_rows(partial_rows, "dp")[0]

    joined_input = ()
    for away in ((0, 1), (2,), (3,)):
        last = away == (3,)
        arrays = []
        for array, _ in join_got if last else [join_got[j * near + i] for j in away for i in range(near)]:
            if not any(array is seen for seen in arrays):
                arrays.append(array)
        at = [[(n, row) for n, seen in enumerate(arrays) if seen is array] for array, row in join_got]
        found = [at[j * near + i][0] for j in away for i in range(near)]
        logs = [one[0] for one in at] if last else []
        out = call(
            functools.partial(place_kernel, groups, capacity, away, found, logs),
            "place_joined",
            [anywhere] * (len(arrays) + len(joined_input)),
            (shape((slots, width), bf16),) + ((shape((slots, kept), bf16), shape((1, slots), f32)) if last else ()),
            (hbm,) + ((vmem, vmem) if last else ()),
            [
                pltpu.VMEM((len(away), count, rows // QUARTERS, packed), bf16),
                pltpu.VMEM((len(away), count, slots // QUARTERS, GROUP), bf16),
                dma((len(away), count, near)),
                dma((len(away), count)),
            ]
            + ([pltpu.VMEM((rows, log_wide), bf16), dma((chips,))] if last else []),
            slots * width * len(away),
            rows * slots * width * len(away),
            aliases={len(arrays): 0} if joined_input else None,
        )(*arrays, *joined_input)
        joined_input = out[:1]
    joined_input, soft_labels, log_partition = out
    return (joined_input, soft_labels, log_partition[0], gain_grad)


def solution(mesh):
    placed = (
        P(("group", "dp"), None),
        P(),
        P(("group", "dp"), None),
        P(("group", "dp"), None),
        P(("group", "dp"), None),
    )
    return jax.shard_map(
        per_device,
        mesh=mesh,
        in_specs=placed,
        out_specs=(
            P(("group", "dp"), None),
            P(("group", "dp"), None),
            P(("group", "dp")),
            P("group", "dp"),
        ),
        check_vma=False,
    )
```
